128 devices in a mesh: row: 16 (over z_lo, y, core), col: 8 (over z_hi, x).
Axes of the slice: x: 4, y: 4, z: 4 (z_hi: 2, z_lo: 2; z = z_hi * 2 + z_lo), core: 2. Of those that a mesh axis runs over, the one named last changes fastest.
Arguments:
- pair_act: bfloat16 [576, 576, 128], P('row', 'col'), may hold values from -6 to 6
- cotangent: bfloat16 [576, 576, 128], P('row', 'col'), may hold values from -6 to 6
- residue_mask: int32 [576], replicated, may hold values 0 or 1
- pair_mask: int32 [576, 576], P('row', 'col'), may hold values 0 or 1
- proj_weight: bfloat16 [128, 512], replicated, may hold values from -0.5 to 0.5
- gate_weight: bfloat16 [128, 128], replicated, may hold values from -0.5 to 0.5
- out_weight: bfloat16 [128, 128], replicated, may hold values from -0.5 to 0.5
- trans_in: bfloat16 [128, 1024], replicated, may hold values from -0.5 to 0.5
- trans_out: bfloat16 [512, 128], replicated, may hold values from -0.25 to 0.25
- norm_gains: float32 [3, 128], replicated, may hold values from 0.1 to 1.9
Outputs:
- grad_pair: bfloat16 [576, 576, 128], P('row', 'col')
- grad_proj: float32 [128, 512], replicated
- grad_gate: float32 [128, 128], replicated
- grad_out: float32 [128, 128], replicated
- grad_trans_in: float32 [128, 1024], replicated
- grad_trans_out: float32 [512, 128], replicated
- grad_gains: float32 [3, 128], replicated
The draws below stay inside these ranges and needn't reach their ends.
All inputs are finite; a program needn't handle non-finite values. No bound on the sum of `pair_mask` on one device may be relied on, other than what follows from the above.
Results may differ from the reference program's by a relative error of at most 0.03.
Values may be sent and summed in bfloat16 or wider, within the bound.
A program may use at most 256 MiB of HBM per device.

```python
import jax
import jax.numpy as jnp
from jax import lax

C = 128
H = 512
ROWS_DEV = 36
N = 576
COLS_DEV = 72
N_COL = 8


def touch_ends(result, key, low, largest):
    spot = [jax.random.randint(jax.random.fold_in(key, axis), (), 0, length) for axis, length in enumerate(result.shape)]
    widest = result.shape.index(max(result.shape))
    next_to = spot[:widest] + [(spot[widest] + 1) % result.shape[widest]] + spot[widest + 1:]
    return result.at[tuple(spot)].set(low).at[tuple(next_to)].set(largest)


def block_scale(own_key, shape, cuts, least, largest):
    loudness, own = 1.0, jax.random.fold_in(own_key, 6)
    for position, blocks in cuts:
        draws = jnp.exp(jax.random.uniform(jax.random.fold_in(own, position), (blocks,), jnp.float32, least / len(cuts), largest / len(cuts)))
        loudness = loudness * jnp.repeat(draws, shape[position] // blocks).reshape([-1 if axis == position else 1 for axis in range(len(shape))])
    return loudness


def centred(key, shape, deviation, bound, split=(), kind=jnp.bfloat16):
    drawn = jax.random.normal(key, shape, jnp.float32) * deviation
    if len(split) > 0:
        drawn = block_scale(key, shape, split, -0.22, 0.18) * drawn
    return jnp.clip(drawn, min=-bound, max=bound).astype(kind)


def setup_inputs(seed: int = 0) -> dict:
    key_of = jax.random.split(jax.random.key(seed), 11)
    return {
        "pair_act": centred(key_of[0], (N, N, C), 1.0, 6.0, ((0, 16), (1, 8))),
        "cotangent": centred(key_of[1], (N, N, C), 1.0, 6.0, ((0, 16), (1, 8))),
        "residue_mask": touch_ends((jax.random.randint(key_of[2], (N,), 0, 8) < 7).astype(jnp.int32), jax.random.fold_in(key_of[2], 1), 0, 1),
        "pair_mask": touch_ends((jax.random.randint(key_of[3], (N, N), 0, 8) < 7).astype(jnp.int32), jax.random.fold_in(key_of[3], 1), 0, 1),
        "proj_weight": centred(key_of[4], (C, 4 * C), C ** -0.5, 0.5),
        "gate_weight": centred(key_of[5], (C, C), C ** -0.5, 0.5),
        "out_weight": centred(key_of[6], (C, C), C ** -0.5, 0.5),
        "trans_in": centred(key_of[7], (C, 2 * H), C ** -0.5, 0.5),
        "trans_out": centred(key_of[8], (H, C), H ** -0.5, 0.25),
        "norm_gains": jnp.clip(1.0 + 0.18 * jax.random.normal(key_of[9], (3, C), jnp.float32), 0.1, 1.9),
    }


EPSILON = 1e-05

def normalize(values):
    center = values - lax.optimization_barrier(jnp.mean(values, axis=-1, keepdims=True))
    inverse = lax.rsqrt(lax.optimization_barrier(jnp.mean(center * center, axis=-1, keepdims=True)) + EPSILON)
    return (center * inverse, inverse)

def normalize_back(grad_hat, normed, inverse):
    mean_grad = lax.optimization_barrier(jnp.mean(grad_hat, axis=-1, keepdims=True))
    second = lax.optimization_barrier(jnp.mean(grad_hat * normed, axis=-1, keepdims=True))
    return inverse * (grad_hat - mean_grad - normed * second)

def over_rows(left_mat, right_mat):
    return lax.dot_general(left_mat, right_mat, (((0,), (0,)), ((), ())), preferred_element_type=jnp.float32)

def over_cols(left_mat, right_mat):
    return lax.dot_general(left_mat, right_mat, (((1,), (1,)), ((), ())), preferred_element_type=jnp.float32)

def project_in(pair_rows, mask_rows, proj_weight, gate_weight, gain_row):
    normed, inverse = normalize(pair_rows.astype(jnp.float32))
    scaled = (normed * gain_row).astype(jnp.bfloat16)
    projected = jnp.dot(scaled, proj_weight, preferred_element_type=jnp.float32)
    channels = gain_row.shape[0]
    left_sig = jax.nn.sigmoid(projected[:, :channels])
    right_sig = jax.nn.sigmoid(projected[:, 2 * channels:3 * channels])
    left_val = (left_sig * projected[:, channels:2 * channels] * mask_rows).astype(jnp.bfloat16)
    right_val = (right_sig * projected[:, 3 * channels:] * mask_rows).astype(jnp.bfloat16)
    gate_val = jax.nn.sigmoid(jnp.dot(scaled, gate_weight, preferred_element_type=jnp.float32))
    return (left_val, right_val, gate_val, projected, scaled, normed, inverse)

def project_out(mixed_rows, gate_val, pair_rows, out_weight, gain_row):
    normed, inverse = normalize(mixed_rows)
    scaled = (normed * gain_row).astype(jnp.bfloat16)
    output = jnp.dot(scaled, out_weight, preferred_element_type=jnp.float32)
    after_mix = (pair_rows.astype(jnp.float32) + gate_val * output).astype(jnp.bfloat16)
    return (after_mix, output, scaled, normed, inverse)

def transition_back(after_mix, cot_rows, trans_in, trans_out, gain_row):
    normed, inverse = normalize(after_mix.astype(jnp.float32))
    scaled = (normed * gain_row).astype(jnp.bfloat16)
    hidden = jnp.dot(scaled, trans_in, preferred_element_type=jnp.float32)
    expand = trans_out.shape[0]
    gate_part = hidden[:, :expand]
    up_part = hidden[:, expand:]
    sigmoid_gate = jax.nn.sigmoid(gate_part)
    swish_gate = gate_part * sigmoid_gate
    inner_act = (swish_gate * up_part).astype(jnp.bfloat16)
    grad_tout = over_rows(inner_act, cot_rows)
    grad_inner = over_cols(cot_rows, trans_out)
    grad_gatepart = grad_inner * up_part * sigmoid_gate * (1.0 + gate_part * (1.0 - sigmoid_gate))
    grad_uppart = grad_inner * swish_gate
    grad_hidden = jnp.concatenate([grad_gatepart, grad_uppart], axis=1).astype(jnp.bfloat16)
    grad_tin = over_rows(scaled, grad_hidden)
    grad_scaled = over_cols(grad_hidden, trans_in)
    grad_gain = lax.optimization_barrier(jnp.sum(grad_scaled * normed, axis=0))
    grad_after = cot_rows.astype(jnp.float32) + normalize_back(grad_scaled * gain_row, normed, inverse)
    return (grad_after, grad_tin, grad_tout, grad_gain)

def output_back(grad_after, gate_val, output, scaled, normed, inverse, out_weight, gain_row):
    grad_output = (grad_after * gate_val).astype(jnp.bfloat16)
    grad_logit = (grad_after * output * gate_val * (1.0 - gate_val)).astype(jnp.bfloat16)
    grad_outw = over_rows(scaled, grad_output)
    grad_scaled = over_cols(grad_output, out_weight)
    grad_gain = lax.optimization_barrier(jnp.sum(grad_scaled * normed, axis=0))
    grad_mixed = normalize_back(grad_scaled * gain_row, normed, inverse).astype(jnp.bfloat16)
    return (grad_mixed, grad_logit, grad_outw, grad_gain)

def input_back(grad_left, grad_right, grad_logit, grad_after, projected, mask_rows, scaled, normed, inverse, proj_weight, gate_weight, gain_row):
    channels = gain_row.shape[0]
    left_sig = jax.nn.sigmoid(projected[:, :channels])
    left_lin = projected[:, channels:2 * channels]
    right_sig = jax.nn.sigmoid(projected[:, 2 * channels:3 * channels])
    right_lin = projected[:, 3 * channels:]
    masked_left = grad_left * mask_rows
    masked_right = grad_right * mask_rows
    grad_proj = jnp.concatenate([masked_left * left_lin * left_sig * (1.0 - left_sig), masked_left * left_sig, masked_right * right_lin * right_sig * (1.0 - right_sig), masked_right * right_sig], axis=1).astype(jnp.bfloat16)
    grad_projw = over_rows(scaled, grad_proj)
    grad_gatew = over_rows(scaled, grad_logit)
    grad_scaled = over_cols(grad_proj, proj_weight) + over_cols(grad_logit, gate_weight)
    grad_gain = lax.optimization_barrier(jnp.sum(grad_scaled * normed, axis=0))
    grad_pair = (grad_after + normalize_back(grad_scaled * gain_row, normed, inverse)).astype(jnp.bfloat16)
    return (grad_pair, grad_projw, grad_gatew, grad_gain)

def reference(pair_act, cotangent, residue_mask, pair_mask, proj_weight, gate_weight, out_weight, trans_in, trans_out, norm_gains):
    residues = pair_act.shape[0]
    channels = pair_act.shape[2]
    blocks = residues // ROWS_DEV
    block_rows = ROWS_DEV * residues
    live_res = residue_mask.astype(jnp.float32)
    full_mask = pair_mask.astype(jnp.float32) * live_res[:, None] * live_res[None, :]
    pair_blocks = pair_act.reshape(blocks, block_rows, channels)
    mask_blocks = full_mask.reshape(blocks, block_rows, 1)
    cot_blocks = cotangent.reshape(blocks, block_rows, channels)

    def first_pass(inputs):
        left_val, right_val, gate_val, projected, scaled, normed, inverse = project_in(inputs[0], inputs[1], proj_weight, gate_weight, norm_gains[0])
        return (left_val, right_val, gate_val)
    left_all, right_all, gate_all = lax.map(first_pass, (pair_blocks, mask_blocks))
    left_grid = left_all.reshape(residues, residues, channels)
    right_grid = right_all.reshape(residues, residues, channels)

    def add_block(block_index, mixed_sum):
        offset = (block_index * COLS_DEV).astype(jnp.int32)
        left_part = lax.dynamic_slice_in_dim(left_grid, offset, COLS_DEV, 1).astype(jnp.float32)
        right_part = lax.dynamic_slice_in_dim(right_grid, offset, COLS_DEV, 1).astype(jnp.float32)
        block_term = jnp.einsum('ikc,jkc->ijc', left_part, right_part, precision=lax.Precision.HIGHEST)
        rounded = lax.optimization_barrier(block_term.astype(jnp.bfloat16))
        return mixed_sum + rounded.astype(jnp.float32)
    mixed_grid = lax.fori_loop(0, N_COL, add_block, jnp.zeros((residues, residues, channels), jnp.float32))
    mixed_blocks = mixed_grid.reshape(blocks, block_rows, channels)

    def second_pass(sums, inputs):
        pair_rows, cot_rows, mixed_rows, gate_rows = inputs
        after_mix, output, scaled, normed, inverse = project_out(mixed_rows, gate_rows, pair_rows, out_weight, norm_gains[1])
        grad_after, grad_tin, grad_tout, gain_three = transition_back(after_mix, cot_rows, trans_in, trans_out, norm_gains[2])
        grad_mixed, grad_logit, grad_outw, gain_two = output_back(grad_after, gate_rows, output, scaled, normed, inverse, out_weight, norm_gains[1])
        sums = (sums[0] + grad_outw, sums[1] + grad_tin, sums[2] + grad_tout, sums[3] + gain_two, sums[4] + gain_three)
        return (sums, (grad_mixed, grad_logit, grad_after))
    initial = (jnp.zeros(out_weight.shape, jnp.float32), jnp.zeros(trans_in.shape, jnp.float32), jnp.zeros(trans_out.shape, jnp.float32), jnp.zeros((channels,), jnp.float32), jnp.zeros((channels,), jnp.float32))
    sums_two, (grad_mixed, grad_logit, grad_after) = lax.scan(second_pass, initial, (pair_blocks, cot_blocks, mixed_blocks, gate_all))
    grad_grid = grad_mixed.reshape(residues, residues, channels).astype(jnp.float32)
    grad_left = jnp.einsum('ijc,jkc->ikc', grad_grid, right_grid.astype(jnp.float32), precision=lax.Precision.HIGHEST)
    grad_right = jnp.einsum('ijc,ikc->jkc', grad_grid, left_grid.astype(jnp.float32), precision=lax.Precision.HIGHEST)

    def third_pass(sums, inputs):
        pair_rows, mask_rows, left_rows, right_rows, logit_rows, after_rows = inputs
        left_val, right_val, gate_val, projected, scaled, normed, inverse = project_in(pair_rows, mask_rows, proj_weight, gate_weight, norm_gains[0])
        grad_pair, grad_projw, grad_gatew, gain_one = input_back(left_rows, right_rows, logit_rows, after_rows, projected, mask_rows, scaled, normed, inverse, proj_weight, gate_weight, norm_gains[0])
        return ((sums[0] + grad_projw, sums[1] + grad_gatew, sums[2] + gain_one), grad_pair)
    start_sums = (jnp.zeros(proj_weight.shape, jnp.float32), jnp.zeros(gate_weight.shape, jnp.float32), jnp.zeros((channels,), jnp.float32))
    sums_three, grad_pairs = lax.scan(third_pass, start_sums, (pair_blocks, mask_blocks, grad_left.reshape(blocks, block_rows, channels), grad_right.reshape(blocks, block_rows, channels), grad_logit, grad_after))
    grad_gains = jnp.stack([sums_three[2], sums_two[3], sums_two[4]]) / residues
    return (grad_pairs.reshape(residues, residues, channels), sums_three[0] / residues, sums_three[1] / residues, sums_two[0] / residues, sums_two[1] / residues, sums_two[2] / residues, grad_gains)
```

```python
import functools

import jax
import jax.numpy as jnp
from jax import lax
from jax.experimental import pallas as pl
from jax.experimental.pallas import tpu as pltpu
from jax.sharding import PartitionSpec as P

EPSILON = 1e-05
BF = jnp.bfloat16
F32 = jnp.float32
MESH = pl.DeviceIdType.MESH
C = 128
NR, NQ = 16, 8
ND = NR * NQ
TI, TK = 36, 72
E = TI * TK
NT = 21
EP = NT * 128
MROWS = TI * NR
KP = NQ * 128
CH = 384
STEPS = EP // CH
LR_T, MX_T = 48, 32
VMEM_LIMIT = 56 * 2**20


def vspec(n):
    return [pl.BlockSpec(memory_space=pltpu.VMEM)] * n


def sds(shape, dtype):
    return jax.ShapeDtypeStruct(shape, dtype)


def sigmoid(v):
    return 0.5 * jnp.tanh(0.5 * v) + 0.5


def norm(v):
    center = v - jnp.mean(v, axis=0, keepdims=True)
    inverse = lax.rsqrt(jnp.mean(center * center, axis=0, keepdims=True) + EPSILON)
    return center * inverse, inverse


def norm_back(h, n, inverse):
    first = jnp.mean(h, axis=0, keepdims=True)
    second = jnp.mean(h * n, axis=0, keepdims=True)
    return inverse * (h - first - n * second)


def mm(a, b):
    return jnp.dot(a, b, preferred_element_type=F32)


def mm_nt(a, b):
    return lax.dot_general(a, b, (((1,), (1,)), ((), ())), preferred_element_type=F32)


def eye():
    return (
        lax.broadcasted_iota(jnp.int32, (C, C), 0) == lax.broadcasted_iota(jnp.int32, (C, C), 1)
    ).astype(BF)


def load_t(ref, off, last):
    if last:
        rows = ref[(STEPS - 1) * CH : E, :]
        rows = jnp.concatenate([rows, jnp.zeros((EP - E, C), rows.dtype)], axis=0)
    else:
        rows = ref[pl.ds(off, CH), :]
    return mm_nt(eye(), rows)


def each_step(body):
    def loop(step, carry):
        body(step, pl.multiple_of(step * CH, CH), False)
        return carry

    lax.fori_loop(0, STEPS - 1, loop, 0)
    body(STEPS - 1, (STEPS - 1) * CH, True)


def gather_rows(ref, base, stride, count):
    return [ref[pl.ds(base + 8 * g * stride, 8, stride=stride), :] for g in range(count // 8)]


def project_kernel(x_ref, live_ref, w_ref, gain_ref, lr_ref, f_ref):
    f_ref[2 * NT * C :, :] = jnp.zeros(((LR_T - 2 * NT) * C, 128), F32)

    def body(step, off, last):
        normed, _ = norm(load_t(x_ref, off, last))
        scaled = (normed * gain_ref[:, 0:1]).astype(BF)
        proj = mm(w_ref[...], scaled)
        live = live_ref[0:1, pl.ds(off, CH)]
        left = sigmoid(proj[0:C]) * proj[C : 2 * C] * live
        right = sigmoid(proj[2 * C : 3 * C]) * proj[3 * C :] * live
        for tt in range(CH // 128):
            t = step * (CH // 128) + tt
            f_ref[pl.ds(t * C, C), :] = left[:, tt * 128 : (tt + 1) * 128]
            f_ref[pl.ds((NT + t) * C, C), :] = right[:, tt * 128 : (tt + 1) * 128]

    each_step(body)

    def out(c, carry):
        lr_ref[c] = jnp.concatenate(gather_rows(f_ref, c, C, LR_T), axis=0).astype(BF)
        return carry

    lax.fori_loop(0, C, out, 0)


def project(x, live, w, gains):
    return pl.pallas_call(
        project_kernel,
        out_shape=sds((C, LR_T, 128), BF),
        in_specs=vspec(4),
        out_specs=pl.BlockSpec(memory_space=pltpu.VMEM),
        scratch_shapes=[pltpu.VMEM((LR_T * C, 128), F32)],
        compiler_params=pltpu.CompilerParams(vmem_limit_bytes=VMEM_LIMIT),
        name="project",
    )(x, live, w, gains)


def middle_kernel(
    x_ref, cot_ref, mix_ref, wg_ref, wo_ref, wot_ref, ti_ref, tit_ref, to_ref, gain_ref,
    g_ref, after_ref, logit_ref, mid_ref,
    f_ref, fo_ref, tin_ref, tout_ref, ow_ref, gw_ref, gn_ref,
):
    H = to_ref.shape[0]

    def unpack(c, carry):
        f_ref[pl.ds(pl.multiple_of(c * MX_T, MX_T), MX_T), :] = mix_ref[c].astype(F32)
        return carry

    lax.fori_loop(0, C, unpack, 0)
    for ref in (tin_ref, tout_ref, ow_ref, gw_ref, gn_ref):
        ref[...] = jnp.zeros_like(ref)
    fo_ref[...] = jnp.zeros_like(fo_ref)

    def body(step, off, last):
        lanes = pl.ds(off, CH)
        x = load_t(x_ref, off, last)
        cot = load_t(cot_ref, off, last)
        cot_b = cot.astype(BF)
        normed_in, _ = norm(x)
        scaled_in = (normed_in * gain_ref[:, 0:1]).astype(BF)
        gate = sigmoid(mm(wg_ref[...], scaled_in))
        mixed = jnp.concatenate(
            [
                jnp.concatenate(gather_rows(f_ref, step * (CH // 128) + tt, MX_T, C), axis=0)
                for tt in range(CH // 128)
            ],
            axis=1,
        )
        normed_x, r_x = norm(mixed)
        scaled_out = (normed_x * gain_ref[:, 1:2]).astype(BF)
        output = mm(wot_ref[...], scaled_out)
        after = (x + gate * output).astype(BF).astype(F32)
        normed_t, r_t = norm(after)
        scaled_t = (normed_t * gain_ref[:, 2:3]).astype(BF)
        hidden = mm(tit_ref[...], scaled_t)
        gpart, upart = hidden[:H], hidden[H:]
        sg = sigmoid(gpart)
        swish = gpart * sg
        inner = (swish * upart).astype(BF)
        tout_ref[...] += mm_nt(inner, cot_b)
        grad_inner = mm(to_ref[...], cot_b)
        grad_hidden = jnp.concatenate(
            [
                (grad_inner * upart * sg * (1.0 + gpart * (1.0 - sg))).astype(BF),
                (grad_inner * swish).astype(BF),
            ],
            axis=0,
        )
        tin_ref[...] += mm_nt(scaled_t, grad_hidden)
        back_t = mm(ti_ref[...], grad_hidden)
        gn_ref[1] += back_t * normed_t
        grad_after = cot + norm_back(back_t * gain_ref[:, 2:3], normed_t, r_t)
        after_ref[:, lanes] = grad_after
        grad_output = (grad_after * gate).astype(BF)
        grad_logit = (grad_after * output * gate * (1.0 - gate)).astype(BF)
        logit_ref[:, lanes] = grad_logit
        gw_ref[...] += mm_nt(scaled_in, grad_logit)
        ow_ref[...] += mm_nt(scaled_out, grad_output)
        back_x = mm(wo_ref[...], grad_output)
        gn_ref[0] += back_x * normed_x
        grad_mixed = norm_back(back_x * gain_ref[:, 1:2], normed_x, r_x)
        for tt in range(CH // 128):
            t = step * (CH // 128) + tt
            for g in range(C // 8):
                fo_ref[pl.ds(t + 8 * g * MX_T, 8, stride=MX_T), :] = grad_mixed[
                    8 * g : 8 * g + 8, tt * 128 : (tt + 1) * 128
                ]

    each_step(body)

    def out(c, carry):
        g_ref[c] = fo_ref[pl.ds(pl.multiple_of(c * MX_T, MX_T), MX_T), :].astype(BF)
        return carry

    lax.fori_loop(0, C, out, 0)
    for b in range(2 * H // C):
        mid_ref[b * C : (b + 1) * C, :] = tin_ref[:, b * C : (b + 1) * C].astype(BF)
    base = 2 * H
    mid_ref[base : base + H, :] = tout_ref[...].astype(BF)
    base += H
    mid_ref[base : base + C, :] = ow_ref[...].astype(BF)
    mid_ref[base + C : base + 2 * C, :] = gw_ref[...].astype(BF)
    base += 2 * C
    mid_ref[base:, :] = jnp.zeros((mid_ref.shape[0] - base, 128), BF)
    rows = [jnp.sum(gn_ref[k].T, axis=0, keepdims=True) for k in range(2)]
    mid_ref[base : base + 16, :] = jnp.concatenate(rows + [jnp.zeros((14, 128), F32)], axis=0).astype(BF)


def middle(x, cot, mix, wg, wo, wot, ti, tit, to, gains):
    return pl.pallas_call(
        middle_kernel,
        out_shape=(sds((C, MX_T, 128), BF), sds((C, EP), F32), sds((C, EP), BF), sds((ND * 16, 128), BF)),
        in_specs=vspec(10),
        out_specs=tuple(vspec(4)),
        scratch_shapes=[
            pltpu.VMEM((MX_T * C, 128), F32),
            pltpu.VMEM((MX_T * C, 128), F32),
            pltpu.VMEM(ti.shape, F32),
            pltpu.VMEM(to.shape, F32),
            pltpu.VMEM((C, C), F32),
            pltpu.VMEM((C, C), F32),
            pltpu.VMEM((2, C, CH), F32),
        ],
        compiler_params=pltpu.CompilerParams(vmem_limit_bytes=VMEM_LIMIT),
        name="middle",
    )(x, cot, mix, wg, wo, wot, ti, tit, to, gains)


def last_kernel(
    x_ref, live_ref, back_ref, logit_ref, after_ref, wt_ref, w_ref, gain_ref,
    pair_ref, tail_ref,
    f_ref, pw_ref, gn_ref,
):
    def unpack(c, carry):
        f_ref[pl.ds(pl.multiple_of(c * LR_T, LR_T), LR_T), :] = back_ref[c].astype(F32)
        return carry

    lax.fori_loop(0, C, unpack, 0)
    pw_ref[...] = jnp.zeros_like(pw_ref)
    gn_ref[...] = jnp.zeros_like(gn_ref)

    def body(step, off, last):
        lanes = pl.ds(off, CH)
        normed, inverse = norm(load_t(x_ref, off, last))
        scaled = (normed * gain_ref[:, 0:1]).astype(BF)
        proj = mm(wt_ref[...], scaled)
        live = live_ref[0:1, lanes]

        def load(base):
            return live * jnp.concatenate(
                [
                    jnp.concatenate(gather_rows(f_ref, base + step * (CH // 128) + tt, LR_T, C), axis=0)
                    for tt in range(CH // 128)
                ],
                axis=1,
            )

        gl, gr = load(0), load(NT)
        s1, s3 = sigmoid(proj[0:C]), sigmoid(proj[2 * C : 3 * C])
        grad_proj = jnp.concatenate(
            [
                (gl * proj[C : 2 * C] * s1 * (1.0 - s1)).astype(BF),
                (gl * s1).astype(BF),
                (gr * proj[3 * C :] * s3 * (1.0 - s3)).astype(BF),
                (gr * s3).astype(BF),
            ],
            axis=0,
        )
        pw_ref[...] += mm_nt(scaled, grad_proj)
        back = mm(w_ref[...], jnp.concatenate([grad_proj, logit_ref[:, lanes]], axis=0))
        gn_ref[...] += back * normed
        grad = after_ref[:, lanes] + norm_back(back * gain_ref[:, 0:1], normed, inverse)
        rows = grad.T.astype(BF)
        if last:
            pair_ref[(STEPS - 1) * CH : E, :] = rows[: E - (STEPS - 1) * CH]
        else:
            pair_ref[pl.ds(off, CH), :] = rows

    each_step(body)
    for b in range(4):
        tail_ref[b * C : (b + 1) * C, :] = pw_ref[:, b * C : (b + 1) * C].astype(BF)
    tail_ref[4 * C :, :] = jnp.zeros((tail_ref.shape[0] - 4 * C, 128), BF)
    tail_ref[4 * C : 4 * C + 16, :] = jnp.concatenate(
        [jnp.sum(gn_ref[...].T, axis=0, keepdims=True), jnp.zeros((15, 128), F32)], axis=0
    ).astype(BF)


def last(x, live, back, logit, after, wt, w, gains):
    return pl.pallas_call(
        last_kernel,
        out_shape=(sds((E, C), BF), sds((ND * 16, 128), BF)),
        in_specs=vspec(8),
        out_specs=tuple(vspec(2)),
        scratch_shapes=[
            pltpu.VMEM((LR_T * C, 128), F32),
            pltpu.VMEM((C, 4 * C), F32),
            pltpu.VMEM((C, CH), F32),
        ],
        compiler_params=pltpu.CompilerParams(vmem_limit_bytes=VMEM_LIMIT),
        name="last",
    )(x, live, back, logit, after, wt, w, gains)


def each_peer(fn):
    r, q = lax.axis_index("row"), lax.axis_index("col")

    def one(pr, dq):
        fn(pr, lax.rem(q + dq, NQ))

    for dq in range(1, NQ):
        one(r, dq)

    def body(dr, carry):
        pr = lax.rem(r + dr, NR)
        for dq in range(NQ):
            one(pr, dq)
        return carry

    lax.fori_loop(1, NR, body, 0)


def entry_barrier():
    barrier = pltpu.get_barrier_semaphore()
    each_peer(
        lambda pr, pq: pl.semaphore_signal(barrier, inc=1, device_id=(pr, pq), device_id_type=MESH)
    )
    pl.semaphore_wait(barrier, ND - 1)


def exchange_start(src, dst, src_slot, dst_slot, sems):
    r, q = lax.axis_index("row"), lax.axis_index("col")
    mine = dst_slot(r, q)

    def send(pr, pq):
        pltpu.make_async_remote_copy(
            src_ref=src.at[src_slot(pr, pq)],
            dst_ref=dst.at[mine],
            send_sem=sems.at[0],
            recv_sem=sems.at[1],
            device_id=(pr, pq),
            device_id_type=MESH,
        ).start()

    each_peer(send)
    pltpu.make_async_copy(src.at[src_slot(r, q)], dst.at[mine], sems.at[2]).start()


def exchange_wait(src, dst, sems):
    part = pl.ds(0, ND - 1)
    pltpu.make_async_copy(src.at[part], dst.at[part], sems.at[1]).wait()
    pltpu.make_async_copy(src.at[0], dst.at[0], sems.at[2]).wait()


def exchange_wait_send(src, dst, sems):
    part = pl.ds(0, ND - 1)
    pltpu.make_async_copy(src.at[part], dst.at[part], sems.at[0]).wait()


def by_channel(r, q):
    return r * NQ + q


def by_entry(r, q):
    return q * NR + r


def widen(src, f_ref, rows):
    def body(s, carry):
        f_ref[pl.ds(pl.multiple_of(s * rows, rows), rows), :] = src[s].astype(F32)
        return carry

    lax.fori_loop(0, ND, body, 0)


def narrow(f_ref, dst, rows):
    def body(s, carry):
        dst[s] = f_ref[pl.ds(pl.multiple_of(s * rows, rows), rows), :].astype(BF)
        return carry

    lax.fori_loop(0, ND, body, 0)


def lane_iota():
    return lax.broadcasted_iota(jnp.int32, (8, 128), 1)


def roll(v, shift):
    shift %= 128
    return v if shift == 0 else pltpu.roll(v, shift, 1)


def split_rows(tiles):
    lane = lane_iota()
    for ii in range(TI):
        t, l = divmod(TK * ii, 128)
        v = tiles[t]
        if l + TK > 128:
            v = jnp.where(lane >= l, v, tiles[t + 1])
        yield ii, jnp.where(lane < TK, roll(v, -l), 0.0)


def join_rows(rows):
    lane = lane_iota()
    rolled = {}
    for t in range(NT):
        first = (128 * t) // TK
        final = min((128 * t + 127) // TK, TI - 1)
        value = jnp.zeros((8, 128), F32)
        for ii in range(final, first - 1, -1):
            start = TK * ii - 128 * t
            if ii not in rolled:
                rolled[ii] = roll(rows(ii), start)
            if ii == final and start + TK < 128:
                value = jnp.where(lane < start + TK, rolled[ii], value)
            elif ii == final:
                value = rolled[ii]
            else:
                value = jnp.where(lane < start + TK, rolled[ii], value)
        yield t, value


def triangle_kernel(lr_ref, mix_ref, l_ref, r_ref, in_ref, f_ref, rf_ref, c_ref, out_ref, sem_a, sem_b):
    entry_barrier()
    exchange_start(lr_ref, in_ref, by_channel, by_entry, sem_a)
    rf_ref[...] = jnp.zeros_like(rf_ref)
    exchange_wait(lr_ref, in_ref, sem_a)
    widen(in_ref, f_ref, LR_T)

    def per_col(q, carry):
        lanes = pl.ds(pl.multiple_of(q * 128, 128), 128)
        halves = []
        for h in range(2):
            base = (q * NR + 8 * h) * LR_T
            tiles = [f_ref[pl.ds(base + t, 8, stride=LR_T), :] for t in range(NT)]
            halves.append([v for _, v in split_rows(tiles)])
        for ii in range(TI):
            l_ref[ii * NR : (ii + 1) * NR, lanes] = jnp.concatenate(
                [halves[0][ii], halves[1][ii]], axis=0
            ).astype(BF)
        for h in range(2):
            base = (q * NR + h) * LR_T + NT
            tiles = [f_ref[pl.ds(base + t, 8, stride=2 * LR_T), :] for t in range(NT)]
            for jj, v in split_rows(tiles):
                rf_ref[pl.ds(h * TI + jj, 8, stride=128), :] = v
        r_ref[:, lanes] = rf_ref[...].astype(BF)
        return carry

    lax.fori_loop(0, NQ, per_col, 0)

    def product(b, carry):
        rows = pl.ds(pl.multiple_of(b * 128, 128), 128)
        c_ref[:, rows] = mm_nt(l_ref[...], r_ref[rows, :])
        return carry

    lax.fori_loop(0, NQ, product, 0)

    def pack(q, carry):
        lanes = pl.ds(pl.multiple_of(q * 128, 128), 128)
        for h in range(2):
            for t, v in join_rows(lambda ii: c_ref[ii * NR + 8 * h : ii * NR + 8 * h + 8, lanes]):
                f_ref[pl.ds((q * NR + 8 * h) * MX_T + t, 8, stride=MX_T), :] = v
        return carry

    lax.fori_loop(0, NQ, pack, 0)
    narrow(f_ref, out_ref, MX_T)
    exchange_start(out_ref, mix_ref, by_entry, by_channel, sem_b)
    exchange_wait_send(lr_ref, in_ref, sem_a)
    exchange_wait(out_ref, mix_ref, sem_b)
    exchange_wait_send(out_ref, mix_ref, sem_b)


def triangle(lr):
    return pl.pallas_call(
        triangle_kernel,
        out_shape=(sds((C, MX_T, 128), BF), sds((MROWS, KP), BF), sds((KP, KP), BF)),
        in_specs=vspec(1),
        out_specs=tuple(vspec(3)),
        scratch_shapes=[
            pltpu.VMEM((ND, LR_T, 128), BF),
            pltpu.VMEM((ND * LR_T, 128), F32),
            pltpu.VMEM((KP, 128), F32),
            pltpu.VMEM((MROWS, KP), F32),
            pltpu.VMEM((ND, MX_T, 128), BF),
            pltpu.SemaphoreType.DMA((3,)),
            pltpu.SemaphoreType.DMA((3,)),
        ],
        compiler_params=pltpu.CompilerParams(
            collective_id=1, has_side_effects=True, vmem_limit_bytes=VMEM_LIMIT
        ),
        name="triangle",
    )(lr)


def triangle_back_kernel(g_ref, l_ref, r_ref, back_ref, in_ref, f_ref, m_ref, c1_ref, c2_ref, out_ref, sem_a, sem_b):
    entry_barrier()
    exchange_start(g_ref, in_ref, by_channel, by_entry, sem_a)
    exchange_wait(g_ref, in_ref, sem_a)
    widen(in_ref, f_ref, MX_T)

    def per_col(q, carry):
        lanes = pl.ds(pl.multiple_of(q * 128, 128), 128)
        halves = []
        for h in range(2):
            base = (q * NR + 8 * h) * MX_T
            tiles = [f_ref[pl.ds(base + t, 8, stride=MX_T), :] for t in range(NT)]
            halves.append([v for _, v in split_rows(tiles)])
        for ii in range(TI):
            m_ref[ii * NR : (ii + 1) * NR, lanes] = jnp.concatenate(
                [halves[0][ii], halves[1][ii]], axis=0
            ).astype(BF)
        return carry

    lax.fori_loop(0, NQ, per_col, 0)

    def product(b, carry):
        lanes = pl.ds(pl.multiple_of(b * 128, 128), 128)
        c1_ref[:, lanes] = mm(m_ref[...], r_ref[:, lanes])
        c2_ref[pl.ds(pl.multiple_of(b * KP, KP), KP), :] = lax.dot_general(
            m_ref[...], l_ref[:, lanes], (((0,), (0,)), ((), ())), preferred_element_type=F32
        )
        return carry

    lax.fori_loop(0, NQ, product, 0)

    def pack(q, carry):
        lanes = pl.ds(pl.multiple_of(q * 128, 128), 128)
        for h in range(2):
            for t, v in join_rows(lambda ii: c1_ref[ii * NR + 8 * h : ii * NR + 8 * h + 8, lanes]):
                f_ref[pl.ds((q * NR + 8 * h) * LR_T + t, 8, stride=LR_T), :] = v
            for t, v in join_rows(lambda jj: c2_ref[pl.ds(q * KP + h * TI + jj, 8, stride=128), :]):
                f_ref[pl.ds((q * NR + h) * LR_T + NT + t, 8, stride=2 * LR_T), :] = v
        return carry

    lax.fori_loop(0, NQ, pack, 0)
    narrow(f_ref, out_ref, LR_T)
    exchange_start(out_ref, back_ref, by_entry, by_channel, sem_b)
    exchange_wait_send(g_ref, in_ref, sem_a)
    exchange_wait(out_ref, back_ref, sem_b)
    exchange_wait_send(out_ref, back_ref, sem_b)


def triangle_back(g, lmat, rmat):
    return pl.pallas_call(
        triangle_back_kernel,
        out_shape=sds((C, LR_T, 128), BF),
        in_specs=vspec(3),
        out_specs=pl.BlockSpec(memory_space=pltpu.VMEM),
        scratch_shapes=[
            pltpu.VMEM((ND, MX_T, 128), BF),
            pltpu.VMEM((ND * LR_T, 128), F32),
            pltpu.VMEM((MROWS, KP), BF),
            pltpu.VMEM((MROWS, KP), F32),
            pltpu.VMEM((NQ * KP, 128), F32),
            pltpu.VMEM((ND, LR_T, 128), BF),
            pltpu.SemaphoreType.DMA((3,)),
            pltpu.SemaphoreType.DMA((3,)),
        ],
        compiler_params=pltpu.CompilerParams(
            collective_id=2, has_side_effects=True, vmem_limit_bytes=VMEM_LIMIT
        ),
        name="triangle_back",
    )(g, lmat, rmat)


def total_kernel(terms_ref, sum_ref, in_ref, own_ref, sem_a, sem_b):
    r, q = lax.axis_index("row"), lax.axis_index("col")
    rows = terms_ref.shape[1]
    entry_barrier()
    exchange_start(terms_ref, in_ref, by_channel, by_channel, sem_a)
    exchange_wait(terms_ref, in_ref, sem_a)
    own = lax.fori_loop(
        0, ND, lambda s, acc: acc + in_ref[s].astype(F32), jnp.zeros((rows, 128), F32)
    )
    own_ref[...] = own.astype(BF)
    mine = by_channel(r, q)

    def send(pr, pq):
        pltpu.make_async_remote_copy(
            src_ref=own_ref,
            dst_ref=sum_ref.at[mine],
            send_sem=sem_b.at[0],
            recv_sem=sem_b.at[1],
            device_id=(pr, pq),
            device_id_type=MESH,
        ).start()

    each_peer(send)
    pltpu.make_async_copy(own_ref, sum_ref.at[mine], sem_b.at[2]).start()
    exchange_wait_send(terms_ref, in_ref, sem_a)
    exchange_wait(in_ref, sum_ref, sem_b)
    exchange_wait_send(in_ref, sum_ref, sem_b)


def total(terms):
    return pl.pallas_call(
        total_kernel,
        out_shape=sds(terms.shape, BF),
        in_specs=vspec(1),
        out_specs=pl.BlockSpec(memory_space=pltpu.VMEM),
        scratch_shapes=[
            pltpu.VMEM(terms.shape, BF),
            pltpu.VMEM(terms.shape[1:], BF),
            pltpu.SemaphoreType.DMA((3,)),
            pltpu.SemaphoreType.DMA((3,)),
        ],
        compiler_params=pltpu.CompilerParams(
            collective_id=3, has_side_effects=True, vmem_limit_bytes=VMEM_LIMIT
        ),
        name="total",
    )(terms)


def on_device(
    pair_act, cotangent, residue_mask, pair_mask, proj_weight, gate_weight, out_weight,
    trans_in, trans_out, norm_gains,
):
    live_res = residue_mask.astype(F32)
    row_live = lax.dynamic_slice_in_dim(live_res, lax.axis_index("row") * TI, TI)
    col_live = lax.dynamic_slice_in_dim(live_res, lax.axis_index("col") * TK, TK)
    live = pair_mask.astype(F32) * row_live[:, None] * col_live[None, :]
    live = jnp.pad(live.reshape(1, E), ((0, 7), (0, EP - E)))
    gains = jnp.pad(norm_gains.T, ((0, 0), (0, 125)))
    x = pair_act.reshape(E, C)
    cot = cotangent.reshape(E, C)
    proj_t = proj_weight.T
    lr = project(x, live, proj_t, gains)
    mix, lmat, rmat = triangle(lr)
    g, after, logit, mid = middle(
        x, cot, mix, gate_weight.T, out_weight, out_weight.T, trans_in, trans_in.T, trans_out, gains
    )
    back = triangle_back(g, lmat, rmat)
    weights = jnp.concatenate([proj_weight, gate_weight], axis=1)
    grad_pair, tail = last(x, live, back, logit, after, proj_t, weights, gains)
    terms = jnp.concatenate([mid.reshape(ND, 16, 128), tail.reshape(ND, 16, 128)], axis=1)
    sums = total(terms).astype(F32) / (TI * NR)
    mid = sums[:, :16].reshape(ND * 16, 128)
    tail = sums[:, 16:].reshape(ND * 16, 128)
    H = trans_out.shape[0]
    tin = mid[: 2 * H].reshape(2 * H // C, C, C).transpose(1, 0, 2).reshape(C, 2 * H)
    tout = mid[2 * H : 3 * H]
    ow = mid[3 * H : 3 * H + C]
    gw = mid[3 * H + C : 3 * H + 2 * C]
    pw = tail[: 4 * C].reshape(4, C, C).transpose(1, 0, 2).reshape(C, 4 * C)
    gains_out = jnp.concatenate([tail[4 * C : 4 * C + 1], mid[3 * H + 2 * C : 3 * H + 2 * C + 2]])
    return grad_pair.reshape(TI, TK, C), pw, gw, ow, tin, tout, gains_out


def solution(mesh):
    split = P("row", "col", None)
    in_specs = (split, split, P(), P("row", "col"), P(), P(), P(), P(), P(), P())
    out_specs = (split, P(), P(), P(), P(), P(), P())
    return jax.shard_map(
        on_device, mesh=mesh, in_specs=in_specs, out_specs=out_specs, check_vma=False
    )
```

```python
import functools

import jax
import jax.numpy as jnp
from jax import lax
from jax.experimental import pallas as pl
from jax.experimental.pallas import tpu as pltpu
from jax.sharding import PartitionSpec as P

EPSILON = 1e-05
BF = jnp.bfloat16
F32 = jnp.float32
MESH = pl.DeviceIdType.MESH
C = 128
NR, NQ = 16, 8
ND = NR * NQ
TI, TK = 36, 72
E = TI * TK
NT = 21
EP = NT * 128
MROWS = TI * NR
KP = NQ * 128
CH = 384
MSG = 16
BLK = (MSG, 128)
A_TILES = 9
A_ROWS = 16
THIRD = 7
OWNERS = 33
VMEM_LIMIT = 60 * 2**20


def vspec(n):
    return [pl.BlockSpec(memory_space=pltpu.VMEM)] * n


def sds(shape, dtype):
    return jax.ShapeDtypeStruct(shape, dtype)


def sigmoid(v):
    return 0.5 * jnp.tanh(0.5 * v) + 0.5


def norm(v):
    center = v - jnp.mean(v, axis=0, keepdims=True)
    inverse = lax.rsqrt(jnp.mean(center * center, axis=0, keepdims=True) + EPSILON)
    return center * inverse, inverse


def norm_back(h, n, inverse):
    first = jnp.mean(h, axis=0, keepdims=True)
    second = jnp.mean(h * n, axis=0, keepdims=True)
    return inverse * (h - first - n * second)


def mm(a, b):
    return jnp.dot(a, b, preferred_element_type=F32)


def mm_nt(a, b):
    return lax.dot_general(a, b, (((1,), (1,)), ((), ())), preferred_element_type=F32)


def eye():
    return (
        lax.broadcasted_iota(jnp.int32, (C, C), 0) == lax.broadcasted_iota(jnp.int32, (C, C), 1)
    ).astype(BF)


def each_peer(fn):
    r, q = lax.axis_index("row"), lax.axis_index("col")

    def one(pr, dq):
        fn(pr, lax.rem(q + dq, NQ))

    for dq in range(1, NQ):
        one(r, dq)

    def body(dr, carry):
        pr = lax.rem(r + dr, NR)
        for dq in range(NQ):
            one(pr, dq)
        return carry

    lax.fori_loop(1, NR, body, 0)


def exchange_start(src, dst, src_slot, dst_slot, sems):
    r, q = lax.axis_index("row"), lax.axis_index("col")
    mine = dst_slot(r, q)

    def send(pr, pq):
        pltpu.make_async_remote_copy(
            src_ref=src.at[src_slot(pr, pq)],
            dst_ref=dst.at[mine],
            send_sem=sems.at[0],
            recv_sem=sems.at[1],
            device_id=(pr, pq),
            device_id_type=MESH,
        ).start()

    each_peer(send)
    pltpu.make_async_copy(src.at[src_slot(r, q)], dst.at[mine], sems.at[2]).start()


def exchange_wait(src, dst, sems):
    part = pl.ds(0, ND - 1)
    pltpu.make_async_copy(src.at[part], dst.at[part], sems.at[1]).wait()
    pltpu.make_async_copy(src.at[0], dst.at[0], sems.at[2]).wait()


def exchange_wait_send(src, dst, sems):
    part = pl.ds(0, ND - 1)
    pltpu.make_async_copy(src.at[part], dst.at[part], sems.at[0]).wait()


def by_channel(r, q):
    return r * NQ + q


def by_entry(r, q):
    return q * NR + r


def chunks(count, fn):
    def loop(i, carry):
        fn(i)
        return carry

    lax.fori_loop(0, count, loop, 0)


def widen(src, f_ref, base=0):
    def some(i):
        f_ref[pl.ds(pl.multiple_of(base + i * 256, 256), 256), :] = (
            src[pl.ds(i * 16, 16)].reshape(256, 128).astype(F32)
        )

    chunks(ND // 16, some)


def narrow(f_ref, dst):
    def some(i):
        dst[pl.ds(i * 16, 16)] = (
            f_ref[pl.ds(pl.multiple_of(i * 256, 256), 256), :].astype(BF).reshape(16, MSG, 128)
        )

    chunks(ND // 16, some)


def lane_iota():
    return lax.broadcasted_iota(jnp.int32, (8, 128), 1)


def roll(v, shift):
    shift %= 128
    return v if shift == 0 else pltpu.roll(v, shift, 1)


def split_rows(tile, rows):
    lane = lane_iota()
    tiles = {}

    def get(t):
        if t not in tiles:
            tiles[t] = tile(t)
        return tiles[t]

    out = []
    for ii in rows:
        t, l = divmod(TK * ii, 128)
        v = get(t)
        if l + TK > 128:
            v = jnp.where(lane >= l, v, get(t + 1))
        out.append((ii, jnp.where(lane < TK, roll(v, -l), 0.0)))
    return out


def join_rows(row, tiles):
    lane = lane_iota()
    rolled = {}
    out = []
    for t in tiles:
        first = (128 * t) // TK
        final = min((128 * t + 127) // TK, TI - 1)
        value = jnp.zeros((8, 128), F32)
        for ii in range(final, first - 1, -1):
            start = TK * ii - 128 * t
            if ii not in rolled:
                rolled[ii] = roll(row(ii), start)
            if ii == final and start + TK >= 128:
                value = rolled[ii]
            else:
                value = jnp.where(lane < start + TK, rolled[ii], value)
        out.append((t, value))
    return out


def put16(ref, ii, lanes, low, high):
    ref[ii * NR : (ii + 1) * NR, lanes] = jnp.concatenate([low, high], axis=0).astype(BF)


def q_lanes(q):
    return pl.ds(pl.multiple_of(q * 128, 128), 128)


def gather_tile(f_ref, base):
    return jnp.concatenate(
        [f_ref[pl.ds(base + 8 * g * MSG, 8, stride=MSG), :] for g in range(C // 8)], axis=0
    )


def sum_blocks(ref):
    def some(i, acc):
        for k in range(8):
            acc = acc + ref[i * 8 + k].astype(F32)
        return acc

    return lax.fori_loop(0, ND // 8, some, jnp.zeros(BLK, F32))


def third_steps(p):
    return ((p * THIRD, 0, 4), (p * THIRD + 4, 4, 3))


def block_kernel(
    x_ref, cot_ref, live_ref, pw_ref, gw_ref, ow_ref, ti_ref, to_ref, gain_ref,
    pair_o, pw_o, gw_o, ow_o, ti_o, to_o, gn_o,
    pwt, gwt, owt, tit, gcol, xt_ref, cott_ref, scaled_ref, proj_ref, gate_ref, gi_ref,
    after_ref, logit_ref, f_ref, fw_ref, l_ref, r_ref, rf_ref, m_ref, mt_ref, c1_ref,
    hid_ref, inner_ref, gh_ref, gp_ref, tin_acc, tout_acc, ow_acc, gw_acc, pw_acc, gn_acc,
    s_a, r_a, s_m, r_m, s_g, r_g, s_b, r_b, s_mid, r_mid, mid_own, mid_sum,
    s_tail, r_tail, tail_own, tail_sum,
    sem_a, sem_m, sem_g, sem_b, sem_mid, sem_mid2, sem_tail, sem_tail2,
):
    H = to_ref.shape[0]
    r, q = lax.axis_index("row"), lax.axis_index("col")
    me = by_channel(r, q)

    barrier = pltpu.get_barrier_semaphore()
    each_peer(
        lambda pr, pq: pl.semaphore_signal(barrier, inc=1, device_id=(pr, pq), device_id_type=MESH)
    )

    def flip(src, dst):
        for b in range(src.shape[1] // C):
            dst[b * C : (b + 1) * C, :] = src[:, b * C : (b + 1) * C].astype(F32).T.astype(BF)

    flip(pw_ref, pwt)
    flip(gw_ref, gwt)
    flip(ow_ref, owt)
    flip(ti_ref, tit)
    gcol[...] = jnp.concatenate([gain_ref[...], jnp.zeros((C - 3, C), F32)], axis=0).T
    gain_in, gain_out, gain_t = (lambda: gcol[:, 0:1]), (lambda: gcol[:, 1:2]), (lambda: gcol[:, 2:3])

    def load_t(ref, t0, nt):
        stop = min((t0 + nt) * 128, E)
        rows = ref[t0 * 128 : stop, :]
        pad = (t0 + nt) * 128 - stop
        if pad:
            rows = jnp.concatenate([rows, jnp.zeros((pad, C), rows.dtype)], axis=0)
        return mm_nt(eye(), rows)

    f_ref[2 * THIRD * C :, :] = jnp.zeros(((MSG - 2 * THIRD) * C, 128), F32)
    for p in range(3):
        for t0, slot, nt in third_steps(p):
            lanes = slice(t0 * 128, (t0 + nt) * 128)
            xt = load_t(x_ref, t0, nt)
            xt_ref[:, lanes] = xt.astype(BF)
            scaled = (norm(xt)[0] * gain_in()).astype(BF)
            scaled_ref[:, lanes] = scaled
            proj_ref[:, lanes] = mm(pwt[...], scaled)
            live = live_ref[0:1, lanes]
            for i in range(0, C, 8):
                left = sigmoid(proj_ref[i : i + 8, lanes]) * proj_ref[C + i : C + i + 8, lanes] * live
                right = (
                    sigmoid(proj_ref[2 * C + i : 2 * C + i + 8, lanes])
                    * proj_ref[3 * C + i : 3 * C + i + 8, lanes]
                    * live
                )
                for tt in range(nt):
                    f_ref[(slot + tt) * C + i : (slot + tt) * C + i + 8, :] = left[:, tt * 128 : tt * 128 + 128]
                    row = (THIRD + slot + tt) * C + i
                    f_ref[row : row + 8, :] = right[:, tt * 128 : tt * 128 + 128]

        def pick(i):
            for k in range(8):
                c = i * 8 + k
                s_a[p, c] = jnp.concatenate(
                    [f_ref[pl.ds(c, 8, stride=C), :], f_ref[pl.ds(8 * C + c, 8, stride=C), :]], axis=0
                ).astype(BF)

        chunks(C // 8, pick)
        if p == 0:
            pl.semaphore_wait(barrier, ND - 1)
        exchange_start(s_a.at[p], r_a.at[p], by_channel, by_entry, sem_a.at[p])

    for ref in (rf_ref, tin_acc, tout_acc, ow_acc, gw_acc, pw_acc, gn_acc):
        ref[...] = jnp.zeros_like(ref)
    for p in range(3):
        for t0, slot, nt in third_steps(p):
            lanes = slice(t0 * 128, (t0 + nt) * 128)
            cot_b = load_t(cot_ref, t0, nt).astype(BF)
            cott_ref[:, lanes] = cot_b
            gate_ref[:, lanes] = sigmoid(mm(gwt[...], scaled_ref[:, lanes]))
            gi_ref[:, lanes] = mm(to_ref[...], cot_b)

    for p in range(3):
        exchange_wait(s_a.at[p], r_a.at[p], sem_a.at[p])
        widen(r_a.at[p], fw_ref, p * ND * MSG)

        def per_col(qq):
            def tile(base, row0, stride):
                return lambda t: fw_ref[
                    pl.ds((t // THIRD) * ND * MSG + base * MSG + row0 + t % THIRD, 8, stride=stride), :
                ]

            rows = range(12 * p, 12 * p + 12)
            low = split_rows(tile(qq * NR, 0, MSG), rows)
            high = split_rows(tile(qq * NR + 8, 0, MSG), rows)
            for (ii, a), (_, b) in zip(low, high):
                put16(l_ref, ii, q_lanes(qq), a, b)
            for h in range(2):
                for jj, v in split_rows(tile(qq * NR + h, THIRD, 2 * MSG), rows):
                    rf_ref[pl.ds(qq * KP + h * TI + jj, 8, stride=128), :] = v
            if p == 2:
                r_ref[:, q_lanes(qq)] = rf_ref[pl.ds(pl.multiple_of(qq * KP, KP), KP), :].astype(BF)

        chunks(NQ, per_col)

    parts = ((0, 0, A_ROWS, 0, A_TILES), (1, A_ROWS, TI, A_TILES, NT))
    for part, i0, i1, t0, t1 in parts:
        rows = slice(i0 * NR, i1 * NR)
        for b in range(0, KP, 256):
            c1_ref[rows, b : b + 256] = mm_nt(l_ref[rows, :], r_ref[b : b + 256, :])

        def pack(qq):
            for h in range(2):
                row = lambda ii: c1_ref[ii * NR + 8 * h : ii * NR + 8 * h + 8, q_lanes(qq)]
                for t, v in join_rows(row, range(t0, t1)):
                    f_ref[pl.ds((qq * NR + 8 * h) * MSG + t - t0, 8, stride=MSG), :] = v

        chunks(NQ, pack)
        narrow(f_ref, s_m.at[part])
        exchange_start(s_m.at[part], r_m.at[part], by_entry, by_channel, sem_m.at[part])

    for part, i0, i1, t0, t1 in parts:
        exchange_wait(s_m.at[part], r_m.at[part], sem_m.at[part])
        widen(r_m.at[part], fw_ref)

        def step(k):
            lanes = pl.ds(pl.multiple_of(t0 * 128 + k * CH, 128), CH)
            mixed = jnp.concatenate([gather_tile(fw_ref, k * 3 + tt) for tt in range(3)], axis=1)
            normed_x, r_x = norm(mixed)
            scaled_out = (normed_x * gain_out()).astype(BF)
            output = mm(owt[...], scaled_out)
            gate = gate_ref[:, lanes]
            after = (xt_ref[:, lanes].astype(F32) + gate * output).astype(BF).astype(F32)
            normed_t, r_t = norm(after)
            scaled_t = (normed_t * gain_t()).astype(BF)
            hid_ref[...] = mm(tit[...], scaled_t)
            for i in range(0, H, 16):
                g = hid_ref[i : i + 16, :]
                u = hid_ref[H + i : H + i + 16, :]
                gi = gi_ref[i : i + 16, lanes]
                sg = sigmoid(g)
                swish = g * sg
                inner_ref[i : i + 16, :] = (swish * u).astype(BF)
                gh_ref[i : i + 16, :] = (gi * u * (sg + swish * (1.0 - sg))).astype(BF)
                gh_ref[H + i : H + i + 16, :] = (gi * swish).astype(BF)
            cot_b = cott_ref[:, lanes]
            back_t = mm(ti_ref[...], gh_ref[...])
            tout_acc[...] += mm_nt(inner_ref[...], cot_b)
            tin_acc[...] += mm_nt(gh_ref[...], scaled_t)
            gn_acc[1, :, :CH] += back_t * normed_t
            grad_after = cot_b.astype(F32) + norm_back(back_t * gain_t(), normed_t, r_t)
            after_ref[:, lanes] = grad_after
            grad_output = (grad_after * gate).astype(BF)
            grad_logit = (grad_after * output * gate * (1.0 - gate)).astype(BF)
            logit_ref[:, lanes] = grad_logit
            gw_acc[...] += mm_nt(scaled_ref[:, lanes], grad_logit)
            ow_acc[...] += mm_nt(scaled_out, grad_output)
            back_x = mm(ow_ref[...], grad_output)
            gn_acc[0, :, :CH] += back_x * normed_x
            grad_mixed = norm_back(back_x * gain_out(), normed_x, r_x)
            for tt in range(3):
                for g in range(C // 8):
                    f_ref[pl.ds(k * 3 + tt + 8 * g * MSG, 8, stride=MSG), :] = grad_mixed[
                        8 * g : 8 * g + 8, tt * 128 : (tt + 1) * 128
                    ]

        chunks((t1 - t0) // 3, step)
        narrow(f_ref, s_g.at[part])
        exchange_start(s_g.at[part], r_g.at[part], by_channel, by_entry, sem_g.at[part])

    def put_terms(dst, first, value):
        n = value.shape[0] // MSG
        dst[first // MSG : first // MSG + n] = value.astype(BF).reshape(n, MSG, 128)

    def gain_rows(values):
        rows = [jnp.sum(v.T, axis=0, keepdims=True) for v in values]
        return jnp.concatenate(rows + [jnp.zeros((MSG - len(rows), 128), F32)], axis=0)

    put_terms(s_mid, 0, tin_acc[...])
    put_terms(s_mid, 2 * H, tout_acc[...])
    put_terms(s_mid, 3 * H, ow_acc[...])
    put_terms(s_mid, 3 * H + C, gw_acc[...])
    rest = 3 * H + 2 * C
    put_terms(s_mid, rest, gain_rows([gn_acc[0], gn_acc[1]]))
    s_mid[rest // MSG + 1 :] = jnp.zeros((ND - rest // MSG - 1, MSG, 128), BF)
    exchange_start(s_mid, r_mid, by_channel, by_channel, sem_mid)

    for part, i0, i1, t0, t1 in parts:
        rows = slice(i0 * NR, i1 * NR)
        exchange_wait(s_g.at[part], r_g.at[part], sem_g.at[part])
        widen(r_g.at[part], fw_ref)

        def per_col(qq):
            def tile(h):
                return lambda t: fw_ref[pl.ds((qq * NR + 8 * h) * MSG + t - t0, 8, stride=MSG), :]

            low, high = split_rows(tile(0), range(i0, i1)), split_rows(tile(1), range(i0, i1))
            for (ii, a), (_, b) in zip(low, high):
                put16(m_ref, ii, q_lanes(qq), a, b)

        chunks(NQ, per_col)
        for b in range(0, KP, 256):
            c1_ref[rows, b : b + 256] = mm(m_ref[rows, :], r_ref[:, b : b + 256])
        for b in range(0, KP, 128):
            mt_ref[b : b + 128, rows] = mm_nt(eye(), m_ref[rows, b : b + 128]).astype(BF)
    for b in range(0, KP, 256):
        both = mm(mt_ref[...], l_ref[:, b : b + 256])
        rf_ref[b // 128 * KP : (b // 128 + 1) * KP, :] = both[:, :128]
        rf_ref[(b // 128 + 1) * KP : (b // 128 + 2) * KP, :] = both[:, 128:]

    for p in range(3):
        tiles = range(p * THIRD, (p + 1) * THIRD)

        def pack(qq):
            for h in range(2):
                row = lambda ii: c1_ref[ii * NR + 8 * h : ii * NR + 8 * h + 8, q_lanes(qq)]
                for t, v in join_rows(row, tiles):
                    f_ref[pl.ds((qq * NR + 8 * h) * MSG + t - p * THIRD, 8, stride=MSG), :] = v
                row = lambda jj: rf_ref[pl.ds(qq * KP + h * TI + jj, 8, stride=128), :]
                for t, v in join_rows(row, tiles):
                    f_ref[pl.ds((qq * NR + h) * MSG + THIRD + t - p * THIRD, 8, stride=2 * MSG), :] = v

        chunks(NQ, pack)
        narrow(f_ref, s_b.at[p])
        exchange_start(s_b.at[p], r_b.at[p], by_entry, by_channel, sem_b.at[p])

    def spread(own, dst, slot, sems):
        def send(pr, pq):
            pltpu.make_async_remote_copy(
                src_ref=own,
                dst_ref=dst.at[slot],
                send_sem=sems.at[0],
                recv_sem=sems.at[1],
                device_id=(pr, pq),
                device_id_type=MESH,
            ).start()

        each_peer(send)
        pltpu.make_async_copy(own, dst.at[slot], sems.at[2]).start()

    exchange_wait(s_mid, r_mid, sem_mid)
    mid_own[...] = sum_blocks(r_mid).astype(BF)
    spread(mid_own, mid_sum, me, sem_mid2)

    for p in range(3):
        exchange_wait(s_b.at[p], r_b.at[p], sem_b.at[p])
        widen(r_b.at[p], fw_ref)
        for t0, slot, nt in third_steps(p):
            w = nt * 128
            lanes = slice(t0 * 128, t0 * 128 + w)
            live = live_ref[0:1, lanes]
            for i in range(0, C, 16):
                def grads(base):
                    return live * jnp.concatenate(
                        [
                            jnp.concatenate(
                                [fw_ref[pl.ds(base + slot + tt + (i + 8 * g) * MSG, 8, stride=MSG), :] for g in range(2)],
                                axis=0,
                            )
                            for tt in range(nt)
                        ],
                        axis=1,
                    )

                for k, base in ((0, 0), (2, THIRD)):
                    grad = grads(base)
                    s = sigmoid(proj_ref[k * C + i : k * C + i + 16, lanes])
                    gs = grad * s
                    gp_ref[(k + 1) * C + i : (k + 1) * C + i + 16, :w] = gs.astype(BF)
                    gp_ref[k * C + i : k * C + i + 16, :w] = (
                        gs * proj_ref[(k + 1) * C + i : (k + 1) * C + i + 16, lanes] * (1.0 - s)
                    ).astype(BF)
            normed, inverse = norm(xt_ref[:, lanes].astype(F32))
            pw_acc[...] += mm_nt(gp_ref[:, :w], scaled_ref[:, lanes])
            back = mm(pw_ref[...], gp_ref[:, :w]) + mm(gw_ref[...], logit_ref[:, lanes])
            prod = back * normed
            gn_acc[2, :, :384] += prod[:, :384]
            if w > 384:
                gn_acc[2, :, 384:w] += prod[:, 384:]
            after_ref[:, lanes] += norm_back(back * gain_in(), normed, inverse)

    put_terms(s_tail, 0, pw_acc[...])
    put_terms(s_tail, 4 * C, gain_rows([gn_acc[2]]))
    even = lax.rem(r, 4) == 0
    odd_one = jnp.logical_and(r == 2, q == 0)
    owner = jnp.logical_or(even, odd_one)
    my_part = jnp.where(even, (r // 4) * NQ + q, OWNERS - 1)

    def tail_send(o, pr, pq):
        remote = jnp.logical_or(pr != r, pq != q)

        @pl.when(remote)
        def _():
            pltpu.make_async_remote_copy(
                src_ref=s_tail.at[o],
                dst_ref=r_tail.at[me],
                send_sem=sem_tail.at[0],
                recv_sem=sem_tail.at[1],
                device_id=(pr, pq),
                device_id_type=MESH,
            ).start()

        @pl.when(jnp.logical_not(remote))
        def _():
            pltpu.make_async_copy(s_tail.at[o], r_tail.at[me], sem_tail.at[2]).start()

    def four(i, carry):
        for k in range(NQ):
            tail_send(i * NQ + k, 4 * i, k)
        return carry

    lax.fori_loop(0, 4, four, 0)
    tail_send(OWNERS - 1, 2, 0)

    for t0 in range(0, NT, 3):
        stop = min((t0 + 3) * 128, E)
        pair_o[t0 * 128 : stop, :] = after_ref[:, t0 * 128 : t0 * 128 + 384].T[: stop - t0 * 128].astype(BF)

    @pl.when(owner)
    def _():
        exchange_wait(r_tail, r_tail, sem_tail)
        tail_own[...] = sum_blocks(r_tail).astype(BF)
        spread(tail_own, tail_sum, my_part, sem_tail2)

    scale = 1.0 / (TI * NR)

    def total(ref, first, rows):
        return ref[first // MSG : (first + rows) // MSG].reshape(rows, 128).astype(F32) * scale

    exchange_wait(r_mid, mid_sum, sem_mid2)
    for b in range(0, 2 * H, C):
        ti_o[:, b : b + C] = total(mid_sum, b, C).T
    to_o[...] = total(mid_sum, 2 * H, H)
    ow_o[...] = total(mid_sum, 3 * H, C)
    gw_o[...] = total(mid_sum, 3 * H + C, C)

    def tail_wait(n):
        pltpu.make_async_copy(r_tail.at[pl.ds(0, n)], r_tail.at[pl.ds(0, n)], sem_tail2.at[1]).wait()

    @pl.when(owner)
    def _():
        tail_wait(OWNERS - 1)
        pltpu.make_async_copy(tail_own, tail_sum.at[0], sem_tail2.at[2]).wait()

    @pl.when(jnp.logical_not(owner))
    def _():
        tail_wait(OWNERS)

    for b in range(0, 4 * C, C):
        pw_o[:, b : b + C] = total(tail_sum, b, C).T
    gn_o[...] = jnp.concatenate(
        [total(tail_sum, 4 * C, MSG)[0:1], total(mid_sum, rest, MSG)[0:2]], axis=0
    )

    for p in range(3):
        exchange_wait_send(s_a.at[p], r_a.at[p], sem_a.at[p])
        exchange_wait_send(s_b.at[p], r_b.at[p], sem_b.at[p])
    for part in range(2):
        exchange_wait_send(s_m.at[part], r_m.at[part], sem_m.at[part])
        exchange_wait_send(s_g.at[part], r_g.at[part], sem_g.at[part])
    exchange_wait_send(s_mid, r_mid, sem_mid)
    exchange_wait_send(r_mid, mid_sum, sem_mid2)

    def tail_left(n, sem):
        pltpu.make_async_copy(r_tail.at[pl.ds(0, n)], r_tail.at[pl.ds(0, n)], sem).wait()

    @pl.when(owner)
    def _():
        tail_left(OWNERS - 1, sem_tail.at[0])
        tail_left(ND - 1, sem_tail2.at[0])

    @pl.when(jnp.logical_not(owner))
    def _():
        tail_left(OWNERS, sem_tail.at[0])


def block(x, cot, live, pw, gw, ow, ti, to, gains):
    H = to.shape[0]
    msgs = lambda *lead: pltpu.VMEM((*lead, ND, MSG, 128), BF)
    dma = lambda *shape: pltpu.SemaphoreType.DMA(shape)
    v = pltpu.VMEM
    return pl.pallas_call(
        block_kernel,
        out_shape=(
            sds((E, C), BF), sds(pw.shape, F32), sds(gw.shape, F32), sds(ow.shape, F32),
            sds(ti.shape, F32), sds(to.shape, F32), sds(gains.shape, F32),
        ),
        in_specs=vspec(9),
        out_specs=tuple(vspec(7)),
        scratch_shapes=[
            v((4 * C, C), BF), v((C, C), BF), v((C, C), BF), v((2 * H, C), BF), v((C, C), F32),
            v((C, EP), BF), v((C, EP), BF), v((C, EP), BF), v((4 * C, EP), F32), v((C, EP), F32),
            v((H, EP), F32), v((C, EP), F32), v((C, EP), BF),
            v((ND * MSG, 128), F32), v((3 * ND * MSG, 128), F32),
            v((MROWS, KP), BF), v((KP, KP), BF), v((NQ * KP, 128), F32), v((MROWS, KP), BF),
            v((KP, MROWS), BF), v((MROWS, KP), F32),
            v((2 * H, CH), F32), v((H, CH), BF), v((2 * H, CH), BF), v((4 * C, 512), BF),
            v((2 * H, C), F32), v((H, C), F32), v((C, C), F32), v((C, C), F32), v((4 * C, C), F32),
            v((3, C, 512), F32),
            msgs(3), msgs(3), msgs(2), msgs(2), msgs(2), msgs(2), msgs(3), msgs(3), msgs(), msgs(),
            v(BLK, BF), msgs(),
            v((OWNERS, *BLK), BF), msgs(), v(BLK, BF), v((OWNERS, *BLK), BF),
            dma(3, 3), dma(2, 3), dma(2, 3), dma(3, 3), dma(3), dma(3), dma(3), dma(3),
        ],
        compiler_params=pltpu.CompilerParams(
            collective_id=1, has_side_effects=True, vmem_limit_bytes=VMEM_LIMIT
        ),
        name="block",
    )(x, cot, live, pw, gw, ow, ti, to, gains)


def on_device(
    pair_act, cotangent, residue_mask, pair_mask, proj_weight, gate_weight, out_weight,
    trans_in, trans_out, norm_gains,
):
    live_res = residue_mask.astype(F32)
    row_live = lax.dynamic_slice_in_dim(live_res, lax.axis_index("row") * TI, TI)
    col_live = lax.dynamic_slice_in_dim(live_res, lax.axis_index("col") * TK, TK)
    live = pair_mask.astype(F32) * row_live[:, None] * col_live[None, :]
    live = jnp.pad(live.reshape(1, E), ((0, 7), (0, EP - E)))
    out = block(
        pair_act.reshape(E, C), cotangent.reshape(E, C), live, proj_weight, gate_weight,
        out_weight, trans_in, trans_out, norm_gains,
    )
    return (out[0].reshape(TI, TK, C), *out[1:])


def solution(mesh):
    split = P("row", "col", None)
    in_specs = (split, split, P(), P("row", "col"), P(), P(), P(), P(), P(), P())
    out_specs = (split, P(), P(), P(), P(), P(), P())
    return jax.shard_map(
        on_device, mesh=mesh, in_specs=in_specs, out_specs=out_specs, check_vma=False
    )
```

```python
import functools

import jax
import jax.numpy as jnp
from jax import lax
from jax.experimental import pallas as pl
from jax.experimental.pallas import tpu as pltpu
from jax.sharding import PartitionSpec as P

EPSILON = 1e-05
BF = jnp.bfloat16
F32 = jnp.float32
MESH = pl.DeviceIdType.MESH
C = 128
NR, NQ = 16, 8
ND = NR * NQ
TI, TK = 36, 72
E = TI * TK
NT = 21
EP = NT * 128
MROWS = TI * NR
KP = NQ * 128
MSG = 16
BLK = (MSG, 128)
G_TILES, G_ROWS = 13, 23
A_ROWS = 16
THIRD = 7
OWNERS = 33
VMEM_LIMIT = 60 * 2**20


def vspec(n):
    return [pl.BlockSpec(memory_space=pltpu.VMEM)] * n


def sds(shape, dtype):
    return jax.ShapeDtypeStruct(shape, dtype)


def sigmoid(v):
    return 0.5 * jnp.tanh(0.5 * v) + 0.5


def norm(v):
    center = v - jnp.mean(v, axis=0, keepdims=True)
    inverse = lax.rsqrt(jnp.mean(center * center, axis=0, keepdims=True) + EPSILON)
    return center * inverse, inverse


def norm_back(h, n, inverse):
    first = jnp.mean(h, axis=0, keepdims=True)
    second = jnp.mean(h * n, axis=0, keepdims=True)
    return inverse * (h - first - n * second)


def mm(a, b):
    return jnp.dot(a, b, preferred_element_type=F32)


def mm_nt(a, b):
    return lax.dot_general(a, b, (((1,), (1,)), ((), ())), preferred_element_type=F32)


def eye():
    return (
        lax.broadcasted_iota(jnp.int32, (C, C), 0) == lax.broadcasted_iota(jnp.int32, (C, C), 1)
    ).astype(BF)


def each_peer(fn):
    r, q = lax.axis_index("row"), lax.axis_index("col")

    def one(pr, dq):
        fn(pr, lax.rem(q + dq, NQ))

    for dq in range(1, NQ):
        one(r, dq)

    def body(dr, carry):
        pr = lax.rem(r + dr, NR)
        for dq in range(NQ):
            one(pr, dq)
        return carry

    lax.fori_loop(1, NR, body, 0)


def exchange_start(src, dst, src_slot, dst_slot, sems):
    r, q = lax.axis_index("row"), lax.axis_index("col")
    mine = dst_slot(r, q)

    def send(pr, pq):
        pltpu.make_async_remote_copy(
            src_ref=src.at[src_slot(pr, pq)],
            dst_ref=dst.at[mine],
            send_sem=sems.at[0],
            recv_sem=sems.at[1],
            device_id=(pr, pq),
            device_id_type=MESH,
        ).start()

    each_peer(send)
    pltpu.make_async_copy(src.at[src_slot(r, q)], dst.at[mine], sems.at[2]).start()


def exchange_wait(src, dst, sems):
    part = pl.ds(0, ND - 1)
    pltpu.make_async_copy(src.at[part], dst.at[part], sems.at[1]).wait()
    pltpu.make_async_copy(src.at[0], dst.at[0], sems.at[2]).wait()


def exchange_wait_send(src, dst, sems):
    part = pl.ds(0, ND - 1)
    pltpu.make_async_copy(src.at[part], dst.at[part], sems.at[0]).wait()


def by_channel(r, q):
    return r * NQ + q


def by_entry(r, q):
    return q * NR + r


def chunks(count, fn):
    def loop(i, carry):
        fn(i)
        return carry

    lax.fori_loop(0, count, loop, 0)


def widen(src, f_ref, base=0):
    rows = src.shape[1]

    def some(i):
        f_ref[pl.ds(pl.multiple_of(base + i * 16 * rows, 128), 16 * rows), :] = (
            src[pl.ds(i * 16, 16)].astype(F32).reshape(16 * rows, 128)
        )

    chunks(ND // 16, some)


def narrow(f_ref, dst):
    rows = dst.shape[1]

    def some(i):
        dst[pl.ds(i * 16, 16)] = (
            f_ref[pl.ds(pl.multiple_of(i * 16 * rows, 128), 16 * rows), :].reshape(16, rows, 128).astype(BF)
        )

    chunks(ND // 16, some)


def lane_iota():
    return lax.broadcasted_iota(jnp.int32, (8, 128), 1)


def roll(v, shift):
    shift %= 128
    return v if shift == 0 else pltpu.roll(v, shift, 1)


def split_rows(tile, rows):
    lane = lane_iota()
    tiles = {}

    def get(t):
        if t not in tiles:
            tiles[t] = tile(t)
        return tiles[t]

    out = []
    for ii in rows:
        t, l = divmod(TK * ii, 128)
        v = get(t)
        if l + TK > 128:
            v = jnp.where(lane >= l, v, get(t + 1))
        out.append((ii, jnp.where(lane < TK, roll(v, -l), 0.0)))
    return out


def join_rows(row, tiles):
    lane = lane_iota()
    rolled = {}
    out = []
    for t in tiles:
        first = (128 * t) // TK
        final = min((128 * t + 127) // TK, TI - 1)
        value = jnp.zeros((8, 128), F32)
        for ii in range(final, first - 1, -1):
            start = TK * ii - 128 * t
            if ii not in rolled:
                rolled[ii] = roll(row(ii), start)
            if ii == final and start + TK >= 128:
                value = rolled[ii]
            else:
                value = jnp.where(lane < start + TK, rolled[ii], value)
        out.append((t, value))
    return out


def put16(ref, ii, lanes, low, high):
    ref[ii * NR : (ii + 1) * NR, lanes] = jnp.concatenate([low, high], axis=0).astype(BF)


def q_lanes(q):
    return pl.ds(pl.multiple_of(q * 128, 128), 128)


def fold(v):
    return sum(v[:, k : k + 128] for k in range(128, v.shape[1], 128)) + v[:, :128]


def sum_blocks(ref):
    def some(i, acc):
        for k in range(8):
            acc = acc + ref[i * 8 + k].astype(F32)
        return acc

    return lax.fori_loop(0, ND // 8, some, jnp.zeros(BLK, F32))


def block_kernel(
    x_ref, cot_ref, live_ref, pw_ref, gw_ref, ow_ref, ti_ref, to_ref, gain_ref,
    pair_o, mid_sum, tail_sum,
    pwt, gwt, owt, tit, gcol, xt_ref, cott_ref, scaled_ref, proj_ref, gate_ref,
    after_ref, logit_ref, f_ref, fw_ref, l_ref, r_ref, rf_ref, m_ref, mt_ref, c1_ref,
    hid_ref, gi_ref, inner_ref, gh_ref, gp_ref, tin_acc, tout_acc, ow_acc, gw_acc, pw_acc, gn_acc,
    s_a, r_a, s_m0, r_m0, s_m1, r_m1, s_g0, r_g0, s_g1, r_g1, s_b2, r_b2, s_b3, r_b3,
    s_mid, r_mid, mid_own,
    s_tail, r_tail, tail_own,
    sem_a, sem_m, sem_g, sem_b, sem_mid, sem_mid2, sem_tail, sem_tail2, entered,
):
    H = to_ref.shape[0]
    r, q = lax.axis_index("row"), lax.axis_index("col")
    me = by_channel(r, q)

    barrier = pltpu.get_barrier_semaphore()

    def greet(sem, pr, pq):
        pl.semaphore_signal(sem, inc=1, device_id=(pr, pq), device_id_type=MESH)

    for d in range(1, NQ):
        greet(barrier, r, lax.rem(q + d, NQ))
    for d in range(1, NR):
        greet(barrier, lax.rem(r + d, NR), q)

    def flip(src, dst):
        for b in range(src.shape[1] // C):
            dst[b * C : (b + 1) * C, :] = src[:, b * C : (b + 1) * C].astype(F32).T.astype(BF)

    flip(pw_ref, pwt)
    gcol[...] = jnp.concatenate([gain_ref[...], jnp.zeros((C - 3, C), F32)], axis=0).T
    gain_in, gain_out, gain_t = (lambda: gcol[:, 0:1]), (lambda: gcol[:, 1:2]), (lambda: gcol[:, 2:3])

    def load_t(ref, t0, nt):
        stop = min((t0 + nt) * 128, E)
        rows = ref[t0 * 128 : stop, :]
        pad = (t0 + nt) * 128 - stop
        if pad:
            rows = jnp.concatenate([rows, jnp.zeros((pad, C), rows.dtype)], axis=0)
        return mm_nt(eye(), rows)

    pl.semaphore_wait(barrier, NR + NQ - 2)
    for d in range(1, NQ):
        greet(entered, r, lax.rem(q + d, NQ))

    f_ref[2 * THIRD * C :, :] = jnp.zeros(((MSG - 2 * THIRD) * C, 128), F32)
    for p in range(3):
        for t0, slot, nt in ((p * THIRD, 0, THIRD),):
            lanes = slice(t0 * 128, (t0 + nt) * 128)
            xt = load_t(x_ref, t0, nt)
            xt_ref[:, lanes] = xt.astype(BF)
            scaled = (norm(xt)[0] * gain_in()).astype(BF)
            scaled_ref[:, lanes] = scaled
            proj_ref[:, lanes] = mm(pwt[...], scaled)
            live = live_ref[0:1, lanes]
            for i in range(0, C, 8):
                left = sigmoid(proj_ref[i : i + 8, lanes]) * proj_ref[C + i : C + i + 8, lanes] * live
                right = (
                    sigmoid(proj_ref[2 * C + i : 2 * C + i + 8, lanes])
                    * proj_ref[3 * C + i : 3 * C + i + 8, lanes]
                    * live
                )
                for tt in range(nt):
                    f_ref[(slot + tt) * C + i : (slot + tt) * C + i + 8, :] = left[:, tt * 128 : tt * 128 + 128]
                    row = (THIRD + slot + tt) * C + i
                    f_ref[row : row + 8, :] = right[:, tt * 128 : tt * 128 + 128]

        def pick(i):
            for k in range(8):
                c = i * 8 + k
                s_a[p, c] = jnp.concatenate(
                    [f_ref[pl.ds(c, 8, stride=C), :], f_ref[pl.ds(8 * C + c, 8, stride=C), :]], axis=0
                ).astype(BF)

        chunks(C // 8, pick)
        if p == 0:
            pl.semaphore_wait(entered, NQ - 1)
        exchange_start(s_a.at[p], r_a.at[p], by_channel, by_entry, sem_a.at[p])

    flip(gw_ref, gwt)
    flip(ow_ref, owt)
    flip(ti_ref, tit)
    for ref in (rf_ref, tin_acc, tout_acc, ow_acc, gw_acc, pw_acc, gn_acc):
        ref[...] = jnp.zeros_like(ref)
    for t0 in range(0, NT, THIRD):
        lanes = slice(t0 * 128, (t0 + THIRD) * 128)
        cott_ref[:, lanes] = load_t(cot_ref, t0, THIRD).astype(BF)
        gate_ref[:, lanes] = sigmoid(mm(gwt[...], scaled_ref[:, lanes]))

    for p in range(3):
        exchange_wait(s_a.at[p], r_a.at[p], sem_a.at[p])
        widen(r_a.at[p], fw_ref, p * ND * MSG)

        def per_col(qq):
            def tile(base, row0, stride):
                return lambda t: fw_ref[
                    pl.ds((t // THIRD) * ND * MSG + base * MSG + row0 + t % THIRD, 8, stride=stride), :
                ]

            rows = range(12 * p, 12 * p + 12)
            low = split_rows(tile(qq * NR, 0, MSG), rows)
            high = split_rows(tile(qq * NR + 8, 0, MSG), rows)
            for (ii, a), (_, b) in zip(low, high):
                put16(l_ref, ii, q_lanes(qq), a, b)
            for h in range(2):
                for jj, v in split_rows(tile(qq * NR + h, THIRD, 2 * MSG), rows):
                    rf_ref[pl.ds(qq * KP + h * TI + jj, 8, stride=128), :] = v
            if p == 2:
                r_ref[:, q_lanes(qq)] = rf_ref[pl.ds(pl.multiple_of(qq * KP, KP), KP), :].astype(BF)

        chunks(NQ, per_col)

    m_parts = ((0, A_ROWS, 0, 8, s_m0, r_m0), (A_ROWS, TI, 8, NT, s_m1, r_m1))
    for k, (i0, i1, t0, t1, src, dst) in enumerate(m_parts):
        rows = slice(i0 * NR, i1 * NR)
        size = src.shape[1]
        for b in range(0, KP, 256):
            c1_ref[rows, b : b + 256] = mm_nt(l_ref[rows, :], r_ref[b : b + 256, :])

        def pack(qq):
            for h in range(2):
                row = lambda ii: c1_ref[ii * NR + 8 * h : ii * NR + 8 * h + 8, q_lanes(qq)]
                for t, v in join_rows(row, range(t0, t1)):
                    f_ref[pl.ds((qq * NR + 8 * h) * size + t - t0, 8, stride=size), :] = v

        chunks(NQ, pack)
        narrow(f_ref, src)
        exchange_start(src, dst, by_entry, by_channel, sem_m.at[k])

    def middle(t0, nt, base, size, out0, out_size):
        w = nt * 128
        lanes = slice(t0 * 128, t0 * 128 + w)
        mixed = jnp.concatenate(
            [
                jnp.concatenate(
                    [fw_ref[pl.ds(base + tt + 8 * g * size, 8, stride=size), :] for g in range(C // 8)],
                    axis=0,
                )
                for tt in range(nt)
            ],
            axis=1,
        )
        normed_x, r_x = norm(mixed)
        scaled_out = (normed_x * gain_out()).astype(BF)
        output = mm(owt[...], scaled_out)
        gate = gate_ref[:, lanes]
        after = (xt_ref[:, lanes].astype(F32) + gate * output).astype(BF).astype(F32)
        normed_t, r_t = norm(after)
        scaled_t = (normed_t * gain_t()).astype(BF)
        cot_b = cott_ref[:, lanes]
        hid_ref[:, :w] = mm(tit[...], scaled_t)
        gi_ref[:, :w] = mm(to_ref[...], cot_b)
        for i in range(0, H, 16):
            g = hid_ref[i : i + 16, :w]
            u = hid_ref[H + i : H + i + 16, :w]
            gi = gi_ref[i : i + 16, :w]
            sg = sigmoid(g)
            swish = g * sg
            inner_ref[i : i + 16, :w] = (swish * u).astype(BF)
            gh_ref[i : i + 16, :w] = (gi * u * (sg + swish * (1.0 - sg))).astype(BF)
            gh_ref[H + i : H + i + 16, :w] = (gi * swish).astype(BF)
        back_t = mm(ti_ref[...], gh_ref[:, :w])
        tout_acc[...] += mm_nt(inner_ref[:, :w], cot_b)
        tin_acc[...] += mm_nt(gh_ref[:, :w], scaled_t)
        gn_acc[1] += fold(back_t * normed_t)
        grad_after = cot_b.astype(F32) + norm_back(back_t * gain_t(), normed_t, r_t)
        after_ref[:, lanes] = grad_after
        grad_output = (grad_after * gate).astype(BF)
        grad_logit = (grad_after * output * gate * (1.0 - gate)).astype(BF)
        logit_ref[:, lanes] = grad_logit
        gw_acc[...] += mm_nt(scaled_ref[:, lanes], grad_logit)
        ow_acc[...] += mm_nt(scaled_out, grad_output)
        back_x = mm(ow_ref[...], grad_output)
        gn_acc[0] += fold(back_x * normed_x)
        grad_mixed = norm_back(back_x * gain_out(), normed_x, r_x)
        for tt in range(nt):
            for g in range(C // 8):
                f_ref[pl.ds(out0 + tt + 8 * g * out_size, 8, stride=out_size), :] = grad_mixed[
                    8 * g : 8 * g + 8, tt * 128 : (tt + 1) * 128
                ]

    exchange_wait(s_m0, r_m0, sem_m.at[0])
    widen(r_m0, fw_ref)
    middle(0, 8, 0, 8, 0, MSG)
    exchange_wait(s_m1, r_m1, sem_m.at[1])
    widen(r_m1, fw_ref)
    middle(8, 5, 0, MSG, 8, MSG)
    narrow(f_ref, s_g0)
    exchange_start(s_g0, r_g0, by_channel, by_entry, sem_g.at[0])
    middle(G_TILES, 8, G_TILES - 8, MSG, 0, 8)
    narrow(f_ref, s_g1)
    exchange_start(s_g1, r_g1, by_channel, by_entry, sem_g.at[1])

    for p in range(3):
        exchange_wait_send(s_a.at[p], r_a.at[p], sem_a.at[p])
    s_b0, s_b1, r_b0, r_b1 = s_a.at[0], s_a.at[1], r_a.at[0], r_a.at[1]
    second = ND * MSG

    def operand(i0, i1):
        def per_col(qq):
            def tile(h):
                first = qq * NR + 8 * h

                def get(t):
                    if t < G_TILES:
                        return fw_ref[pl.ds(first * MSG + t, 8, stride=MSG), :]
                    return fw_ref[pl.ds(second + first * 8 + t - G_TILES, 8, stride=8), :]

                return get

            low, high = split_rows(tile(0), range(i0, i1)), split_rows(tile(1), range(i0, i1))
            for (ii, a), (_, b) in zip(low, high):
                put16(m_ref, ii, q_lanes(qq), a, b)

        chunks(NQ, per_col)
        rows = slice(i0 * NR, i1 * NR)
        for b in range(0, KP, 256):
            c1_ref[rows, b : b + 256] = mm(m_ref[rows, :], r_ref[:, b : b + 256])

    def pack_left(tiles, row0, size):
        def pack(qq):
            for h in range(2):
                row = lambda ii: c1_ref[ii * NR + 8 * h : ii * NR + 8 * h + 8, q_lanes(qq)]
                for t, v in join_rows(row, tiles):
                    f_ref[pl.ds((qq * NR + 8 * h) * size + row0 + t - tiles[0], 8, stride=size), :] = v

        chunks(NQ, pack)

    def pack_right(tiles, row0, size):
        def pack(qq):
            for h in range(2):
                row = lambda jj: rf_ref[pl.ds(qq * KP + h * TI + jj, 8, stride=128), :]
                for t, v in join_rows(row, tiles):
                    at = pl.ds((qq * NR + h) * size + row0 + t - tiles[0], 8, stride=2 * size)
                    f_ref[at, :] = v

        chunks(NQ, pack)

    exchange_wait(s_g0, r_g0, sem_g.at[0])
    widen(r_g0, fw_ref)
    operand(0, G_ROWS)
    pack_left(range(0, 12), 0, MSG)
    narrow(f_ref, s_b0)
    exchange_start(s_b0, r_b0, by_entry, by_channel, sem_b.at[0])

    def put_terms(dst, first, value):
        n = value.shape[0] // MSG
        dst[first // MSG : first // MSG + n] = value.astype(BF).reshape(n, MSG, 128)

    def gain_rows(values):
        rows = [jnp.sum(v.T, axis=0, keepdims=True) for v in values]
        return jnp.concatenate(rows + [jnp.zeros((MSG - len(rows), 128), F32)], axis=0)

    put_terms(s_mid, 0, tin_acc[...])
    put_terms(s_mid, 2 * H, tout_acc[...])
    put_terms(s_mid, 3 * H, ow_acc[...])
    put_terms(s_mid, 3 * H + C, gw_acc[...])
    rest = 3 * H + 2 * C
    put_terms(s_mid, rest, gain_rows([gn_acc[0], gn_acc[1]]))
    s_mid[rest // MSG + 1 :] = jnp.zeros((ND - rest // MSG - 1, MSG, 128), BF)
    exchange_start(s_mid, r_mid, by_channel, by_channel, sem_mid)

    exchange_wait(s_g1, r_g1, sem_g.at[1])
    widen(r_g1, fw_ref, second)
    operand(G_ROWS, TI)
    for b in range(0, KP, 128):
        mt_ref[b : b + 128, :] = mm_nt(eye(), m_ref[:, b : b + 128]).astype(BF)
    for b in range(0, KP, 256):
        both = mm(mt_ref[...], l_ref[:, b : b + 256])
        rf_ref[b // 128 * KP : (b // 128 + 1) * KP, :] = both[:, :128]
        rf_ref[(b // 128 + 1) * KP : (b // 128 + 2) * KP, :] = both[:, 128:]
    pack_left(range(12, NT), 0, MSG)
    pack_right(range(0, 7), 9, MSG)
    narrow(f_ref, s_b1)
    exchange_start(s_b1, r_b1, by_entry, by_channel, sem_b.at[1])
    pack_right(range(7, 15), 0, 8)
    narrow(f_ref, s_b2)
    exchange_start(s_b2, r_b2, by_entry, by_channel, sem_b.at[2])
    pack_right(range(15, NT), 0, 8)
    narrow(f_ref, s_b3)
    exchange_start(s_b3, r_b3, by_entry, by_channel, sem_b.at[3])

    def spread(own, dst, slot, sems):
        def send(pr, pq):
            pltpu.make_async_remote_copy(
                src_ref=own,
                dst_ref=dst.at[slot],
                send_sem=sems.at[0],
                recv_sem=sems.at[1],
                device_id=(pr, pq),
                device_id_type=MESH,
            ).start()

        each_peer(send)
        pltpu.make_async_copy(own, dst.at[slot], sems.at[2]).start()

    exchange_wait(s_mid, r_mid, sem_mid)
    mid_own[...] = sum_blocks(r_mid).astype(BF)
    spread(mid_own, mid_sum, me, sem_mid2)

    def left_at(t):
        return (t, MSG) if t < 12 else (second + t - 12, MSG)

    def right_at(t):
        if t < 7:
            return (second + 9 + t, MSG)
        return (2 * second + t - 7, 8) if t < 15 else (2 * second + ND * 8 + t - 15, 8)

    def project_back(t0, nt):
        w = nt * 128
        lanes = slice(t0 * 128, t0 * 128 + w)
        live = live_ref[0:1, lanes]
        for i in range(0, C, 16):
            for k, at in ((0, left_at), (2, right_at)):
                grad = []
                for t in range(t0, t0 + nt):
                    base, size = at(t)
                    grad.append(
                        jnp.concatenate(
                            [fw_ref[pl.ds(base + (i + 8 * g) * size, 8, stride=size), :] for g in range(2)],
                            axis=0,
                        )
                    )
                s = sigmoid(proj_ref[k * C + i : k * C + i + 16, lanes])
                gs = live * jnp.concatenate(grad, axis=1) * s
                gp_ref[(k + 1) * C + i : (k + 1) * C + i + 16, :w] = gs.astype(BF)
                gp_ref[k * C + i : k * C + i + 16, :w] = (
                    gs * proj_ref[(k + 1) * C + i : (k + 1) * C + i + 16, lanes] * (1.0 - s)
                ).astype(BF)
        normed, inverse = norm(xt_ref[:, lanes].astype(F32))
        pw_acc[...] += mm_nt(gp_ref[:, :w], scaled_ref[:, lanes])
        back = mm(pw_ref[...], gp_ref[:, :w]) + mm(gw_ref[...], logit_ref[:, lanes])
        gn_acc[2] += fold(back * normed)
        after_ref[:, lanes] += norm_back(back * gain_in(), normed, inverse)

    exchange_wait(s_b0, r_b0, sem_b.at[0])
    widen(r_b0, fw_ref)
    exchange_wait(s_b1, r_b1, sem_b.at[1])
    widen(r_b1, fw_ref, second)
    project_back(0, 7)
    exchange_wait(s_b2, r_b2, sem_b.at[2])
    widen(r_b2, fw_ref, 2 * second)
    project_back(7, 8)
    exchange_wait(s_b3, r_b3, sem_b.at[3])
    widen(r_b3, fw_ref, 2 * second + ND * 8)
    project_back(15, 6)

    put_terms(s_tail, 0, pw_acc[...])
    put_terms(s_tail, 4 * C, gain_rows([gn_acc[2]]))
    even = lax.rem(r, 4) == 0
    odd_one = jnp.logical_and(r == 2, q == 0)
    owner = jnp.logical_or(even, odd_one)
    my_part = jnp.where(even, (r // 4) * NQ + q, OWNERS - 1)

    def tail_send(o, pr, pq):
        remote = jnp.logical_or(pr != r, pq != q)

        @pl.when(remote)
        def _():
            pltpu.make_async_remote_copy(
                src_ref=s_tail.at[o],
                dst_ref=r_tail.at[me],
                send_sem=sem_tail.at[0],
                recv_sem=sem_tail.at[1],
                device_id=(pr, pq),
                device_id_type=MESH,
            ).start()

        @pl.when(jnp.logical_not(remote))
        def _():
            pltpu.make_async_copy(s_tail.at[o], r_tail.at[me], sem_tail.at[2]).start()

    def four(i, carry):
        for k in range(NQ):
            tail_send(i * NQ + k, 4 * i, k)
        return carry

    lax.fori_loop(0, 4, four, 0)
    tail_send(OWNERS - 1, 2, 0)

    for t0 in range(0, NT, 3):
        stop = min((t0 + 3) * 128, E)
        pair_o[t0 * 128 : stop, :] = after_ref[:, t0 * 128 : t0 * 128 + 384].T[: stop - t0 * 128].astype(BF)

    @pl.when(owner)
    def _():
        exchange_wait(r_tail, r_tail, sem_tail)
        tail_own[...] = sum_blocks(r_tail).astype(BF)
        spread(tail_own, tail_sum, my_part, sem_tail2)

    exchange_wait(r_mid, mid_sum, sem_mid2)
    def tail_wait(n):
        pltpu.make_async_copy(r_tail.at[pl.ds(0, n)], r_tail.at[pl.ds(0, n)], sem_tail2.at[1]).wait()

    @pl.when(owner)
    def _():
        tail_wait(OWNERS - 1)
        pltpu.make_async_copy(tail_own, tail_sum.at[0], sem_tail2.at[2]).wait()

    @pl.when(jnp.logical_not(owner))
    def _():
        tail_wait(OWNERS)

    for k, (src, dst) in enumerate(((s_m0, r_m0), (s_m1, r_m1))):
        exchange_wait_send(src, dst, sem_m.at[k])
    for k, (src, dst) in enumerate(((s_g0, r_g0), (s_g1, r_g1))):
        exchange_wait_send(src, dst, sem_g.at[k])
    for k, (src, dst) in enumerate(((s_b0, r_b0), (s_b1, r_b1), (s_b2, r_b2), (s_b3, r_b3))):
        exchange_wait_send(src, dst, sem_b.at[k])
    exchange_wait_send(s_mid, r_mid, sem_mid)
    exchange_wait_send(r_mid, mid_sum, sem_mid2)

    def tail_left(n, sem):
        pltpu.make_async_copy(r_tail.at[pl.ds(0, n)], r_tail.at[pl.ds(0, n)], sem).wait()

    @pl.when(owner)
    def _():
        tail_left(OWNERS - 1, sem_tail.at[0])
        tail_left(ND - 1, sem_tail2.at[0])

    @pl.when(jnp.logical_not(owner))
    def _():
        tail_left(OWNERS, sem_tail.at[0])


def block(x, cot, live, pw, gw, ow, ti, to, gains):
    H = to.shape[0]
    wide = 1024
    msgs = lambda rows, *lead: pltpu.VMEM((*lead, ND, rows, 128), BF)
    dma = lambda *shape: pltpu.SemaphoreType.DMA(shape)
    v = pltpu.VMEM
    return pl.pallas_call(
        block_kernel,
        out_shape=(sds((E, C), BF), sds((ND, *BLK), BF), sds((OWNERS, *BLK), BF)),
        in_specs=vspec(9),
        out_specs=tuple(vspec(3)),
        scratch_shapes=[
            v((4 * C, C), BF), v((C, C), BF), v((C, C), BF), v((2 * H, C), BF), v((C, C), F32),
            v((C, EP), BF), v((C, EP), BF), v((C, EP), BF), v((4 * C, EP), F32), v((C, EP), F32),
            v((C, EP), F32), v((C, EP), BF),
            v((ND * MSG, 128), F32), v((3 * ND * MSG, 128), F32),
            v((MROWS, KP), BF), v((KP, KP), BF), v((NQ * KP, 128), F32), v((MROWS, KP), BF),
            v((KP, MROWS), BF), v((MROWS, KP), F32),
            v((2 * H, wide), F32), v((H, wide), F32), v((H, wide), BF), v((2 * H, wide), BF),
            v((4 * C, wide), BF),
            v((2 * H, C), F32), v((H, C), F32), v((C, C), F32), v((C, C), F32), v((4 * C, C), F32),
            v((3, C, 128), F32),
            msgs(16, 3), msgs(16, 3), msgs(8), msgs(8), msgs(16), msgs(16), msgs(16), msgs(16),
            msgs(8), msgs(8), msgs(8), msgs(8), msgs(8), msgs(8),
            msgs(16), msgs(16), v(BLK, BF),
            v((OWNERS, *BLK), BF), msgs(16), v(BLK, BF),
            dma(3, 3), dma(2, 3), dma(2, 3), dma(4, 3), dma(3), dma(3), dma(3), dma(3),
            pltpu.SemaphoreType.REGULAR,
        ],
        compiler_params=pltpu.CompilerParams(
            collective_id=1, has_side_effects=True, vmem_limit_bytes=VMEM_LIMIT
        ),
        name="block",
    )(x, cot, live, pw, gw, ow, ti, to, gains)


def finish_kernel(pair_ref, mid_ref, tail_ref, pair_o, pw_o, gw_o, ow_o, ti_o, to_o, gn_o):
    H = to_o.shape[0]
    scale = 1.0 / (TI * NR)

    def total(ref, first, rows):
        return ref[first // MSG : (first + rows) // MSG].astype(F32).reshape(rows, 128) * scale

    pair_o[...] = pair_ref[...]
    for b in range(0, 2 * H, C):
        ti_o[:, b : b + C] = total(mid_ref, b, C).T
    to_o[...] = total(mid_ref, 2 * H, H)
    ow_o[...] = total(mid_ref, 3 * H, C)
    gw_o[...] = total(mid_ref, 3 * H + C, C)
    for b in range(0, 4 * C, C):
        pw_o[:, b : b + C] = total(tail_ref, b, C).T
    gn_o[...] = jnp.concatenate(
        [total(tail_ref, 4 * C, MSG)[0:1], total(mid_ref, 3 * H + 2 * C, MSG)[0:2]], axis=0
    )


def finish(pair, mid, tail, pw, gw, ow, ti, to, gains):
    return pl.pallas_call(
        finish_kernel,
        out_shape=(
            sds((E, C), BF), sds(pw.shape, F32), sds(gw.shape, F32), sds(ow.shape, F32),
            sds(ti.shape, F32), sds(to.shape, F32), sds(gains.shape, F32),
        ),
        in_specs=vspec(3),
        out_specs=tuple(vspec(7)),
        name="finish",
    )(pair, mid, tail)


def on_device(
    pair_act, cotangent, residue_mask, pair_mask, proj_weight, gate_weight, out_weight,
    trans_in, trans_out, norm_gains,
):
    live_res = residue_mask.astype(F32)
    row_live = lax.dynamic_slice_in_dim(live_res, lax.axis_index("row") * TI, TI)
    col_live = lax.dynamic_slice_in_dim(live_res, lax.axis_index("col") * TK, TK)
    live = pair_mask.astype(F32) * row_live[:, None] * col_live[None, :]
    live = jnp.pad(live.reshape(1, E), ((0, 7), (0, EP - E)))
    weights = (proj_weight, gate_weight, out_weight, trans_in, trans_out, norm_gains)
    sums = block(pair_act.reshape(E, C), cotangent.reshape(E, C), live, *weights)
    out = finish(*sums, *weights)
    return (out[0].reshape(TI, TK, C), *out[1:])


def solution(mesh):
    split = P("row", "col", None)
    in_specs = (split, split, P(), P("row", "col"), P(), P(), P(), P(), P(), P())
    out_specs = (split, P(), P(), P(), P(), P(), P())
    return jax.shard_map(
        on_device, mesh=mesh, in_specs=in_specs, out_specs=out_specs, check_vma=False
    )
```

```python
import functools

import jax
import jax.numpy as jnp
from jax import lax
from jax.experimental import pallas as pl
from jax.experimental.pallas import tpu as pltpu
from jax.sharding import PartitionSpec as P

EPSILON = 1e-05
BF = jnp.bfloat16
F32 = jnp.float32
MESH = pl.DeviceIdType.MESH
C = 128
NR, NQ = 16, 8
ND = NR * NQ
TI, TK = 36, 72
E = TI * TK
NT = 21
EP = NT * 128
MROWS = TI * NR
KP = NQ * 128
MSG = 16
HALF = ND // 2
G_TILES, G_ROWS = 13, 23
A_ROWS = 16
THIRD = 7
VMEM_LIMIT = 60 * 2**20


def vspec(n):
    return [pl.BlockSpec(memory_space=pltpu.VMEM)] * n


def sds(shape, dtype):
    return jax.ShapeDtypeStruct(shape, dtype)


def sigmoid(v):
    return 0.5 * jnp.tanh(0.5 * v) + 0.5


def norm(v):
    center = v - jnp.mean(v, axis=0, keepdims=True)
    inverse = lax.rsqrt(jnp.mean(center * center, axis=0, keepdims=True) + EPSILON)
    return center * inverse, inverse


def norm_back(h, n, inverse):
    first = jnp.mean(h, axis=0, keepdims=True)
    second = jnp.mean(h * n, axis=0, keepdims=True)
    return inverse * (h - first - n * second)


def mm(a, b):
    return jnp.dot(a, b, preferred_element_type=F32)


def mm_nt(a, b):
    return lax.dot_general(a, b, (((1,), (1,)), ((), ())), preferred_element_type=F32)


def eye():
    return (
        lax.broadcasted_iota(jnp.int32, (C, C), 0) == lax.broadcasted_iota(jnp.int32, (C, C), 1)
    ).astype(BF)


def each_peer(fn):
    r, q = lax.axis_index("row"), lax.axis_index("col")

    cols = [lax.rem(q + dq, NQ) for dq in range(NQ)]

    def one(pr, dq):
        fn(pr, cols[dq])

    for dq in range(1, NQ):
        one(r, dq)

    def body(dr, carry):
        pr = lax.rem(r + dr, NR)
        for dq in range(NQ):
            one(pr, dq)
        return carry

    lax.fori_loop(1, NR, body, 0)


def exchange_start(src, dst, src_slot, dst_slot, sems):
    r, q = lax.axis_index("row"), lax.axis_index("col")
    mine = dst_slot(r, q)

    def send(pr, pq):
        pltpu.make_async_remote_copy(
            src_ref=src.at[src_slot(pr, pq)],
            dst_ref=dst.at[mine],
            send_sem=sems.at[0],
            recv_sem=sems.at[1],
            device_id=(pr, pq),
            device_id_type=MESH,
        ).start()

    each_peer(send)
    pltpu.make_async_copy(src.at[src_slot(r, q)], dst.at[mine], sems.at[2]).start()


def exchange_wait(src, dst, sems):
    part = pl.ds(0, ND - 1)
    pltpu.make_async_copy(src.at[part], dst.at[part], sems.at[1]).wait()
    pltpu.make_async_copy(src.at[0], dst.at[0], sems.at[2]).wait()


def exchange_wait_send(src, dst, sems):
    part = pl.ds(0, ND - 1)
    pltpu.make_async_copy(src.at[part], dst.at[part], sems.at[0]).wait()


def by_channel(r, q):
    return r * NQ + q


def by_entry(r, q):
    return q * NR + r


def chunks(count, fn):
    def loop(i, carry):
        fn(i)
        return carry

    lax.fori_loop(0, count, loop, 0)


def widen(src, f_ref, base=0):
    rows = src.shape[1]

    def some(i):
        f_ref[pl.ds(pl.multiple_of(base + i * 16 * rows, 128), 16 * rows), :] = (
            src[pl.ds(i * 16, 16)].astype(F32).reshape(16 * rows, 128)
        )

    chunks(ND // 16, some)


def narrow(f_ref, dst):
    rows = dst.shape[1]

    def some(i):
        dst[pl.ds(i * 16, 16)] = (
            f_ref[pl.ds(pl.multiple_of(i * 16 * rows, 128), 16 * rows), :].reshape(16, rows, 128).astype(BF)
        )

    chunks(ND // 16, some)


def lane_iota():
    return lax.broadcasted_iota(jnp.int32, (8, 128), 1)


def roll(v, shift):
    shift %= 128
    return v if shift == 0 else pltpu.roll(v, shift, 1)


def split_rows(tile, rows):
    lane = lane_iota()
    tiles = {}

    def get(t):
        if t not in tiles:
            tiles[t] = tile(t)
        return tiles[t]

    out = []
    for ii in rows:
        t, l = divmod(TK * ii, 128)
        v = get(t)
        if l + TK > 128:
            v = jnp.where(lane >= l, v, get(t + 1))
        out.append((ii, jnp.where(lane < TK, roll(v, -l), 0.0)))
    return out


def join_rows(row, tiles):
    lane = lane_iota()
    rolled = {}
    out = []
    for t in tiles:
        first = (128 * t) // TK
        final = min((128 * t + 127) // TK, TI - 1)
        value = jnp.zeros((8, 128), F32)
        for ii in range(final, first - 1, -1):
            start = TK * ii - 128 * t
            if ii not in rolled:
                rolled[ii] = roll(row(ii), start)
            if ii == final and start + TK >= 128:
                value = rolled[ii]
            else:
                value = jnp.where(lane < start + TK, rolled[ii], value)
        out.append((t, value))
    return out


def put16(ref, ii, lanes, low, high):
    ref[ii * NR : (ii + 1) * NR, lanes] = jnp.concatenate([low, high], axis=0).astype(BF)


def q_lanes(q):
    return pl.ds(pl.multiple_of(q * 128, 128), 128)


def fold(v):
    return sum(v[:, k : k + 128] for k in range(128, v.shape[1], 128)) + v[:, :128]


def add_blocks(ref, dst):
    total = ref[0].astype(F32)
    for k in range(1, ref.shape[0]):
        total = total + ref[k].astype(F32)
    dst[...] = total.astype(BF)


def block_kernel(
    x_ref, cot_ref, live_ref, pw_ref, gw_ref, ow_ref, ti_ref, to_ref, gain_ref,
    pair_o, mid_sum, tail_sum,
    pwt, gwt, owt, tit, gcol, xt_ref, cott_ref, scaled_ref, proj_ref, gate_ref,
    after_ref, logit_ref, f_ref, fw_ref, l_ref, r_ref, rf_ref, m_ref, mt_ref, c1_ref,
    hid_ref, gi_ref, inner_ref, gh_ref, gp_ref, tin_acc, tout_acc, ow_acc, gw_acc, pw_acc, gn_acc,
    s_a, r_a, s_m0, r_m0, s_m1, r_m1, s_g0, r_g0, s_g1, r_g1, s_b2, r_b2, s_b3, r_b3,
    s_mid, h_mid, p_mid, r_mid, own_mid,
    s_tail, r_tail, row_tail, q_tail, all_tail,
    sem_a, sem_m, sem_g, sem_b, sem_mid, sem_tail, entered,
):
    H = to_ref.shape[0]
    r, q = lax.axis_index("row"), lax.axis_index("col")
    me = by_channel(r, q)

    barrier = pltpu.get_barrier_semaphore()

    def greet(sem, pr, pq):
        pl.semaphore_signal(sem, inc=1, device_id=(pr, pq), device_id_type=MESH)

    for d in range(1, NQ):
        greet(barrier, r, lax.rem(q + d, NQ))
    for d in range(1, NR):
        greet(barrier, lax.rem(r + d, NR), q)

    def flip(src, dst):
        for b in range(src.shape[1] // C):
            dst[b * C : (b + 1) * C, :] = src[:, b * C : (b + 1) * C].astype(F32).T.astype(BF)

    flip(pw_ref, pwt)
    gcol[...] = jnp.concatenate([gain_ref[...], jnp.zeros((C - 3, C), F32)], axis=0).T
    gain_in, gain_out, gain_t = (lambda: gcol[:, 0:1]), (lambda: gcol[:, 1:2]), (lambda: gcol[:, 2:3])

    def load_t(ref, t0, nt):
        stop = min((t0 + nt) * 128, E)
        rows = ref[t0 * 128 : stop, :]
        pad = (t0 + nt) * 128 - stop
        if pad:
            rows = jnp.concatenate([rows, jnp.zeros((pad, C), rows.dtype)], axis=0)
        return mm_nt(eye(), rows)

    pl.semaphore_wait(barrier, NR + NQ - 2)
    for d in range(1, NQ):
        greet(entered, r, lax.rem(q + d, NQ))

    f_ref[2 * THIRD * C :, :] = jnp.zeros(((MSG - 2 * THIRD) * C, 128), F32)
    for p in range(3):
        for t0, slot, nt in ((p * THIRD, 0, THIRD),):
            lanes = slice(t0 * 128, (t0 + nt) * 128)
            xt = load_t(x_ref, t0, nt)
            xt_ref[:, lanes] = xt.astype(BF)
            scaled = (norm(xt)[0] * gain_in()).astype(BF)
            scaled_ref[:, lanes] = scaled
            proj_ref[:, lanes] = mm(pwt[...], scaled)
            live = live_ref[0:1, lanes]
            for i in range(0, C, 8):
                left = sigmoid(proj_ref[i : i + 8, lanes]) * proj_ref[C + i : C + i + 8, lanes] * live
                right = (
                    sigmoid(proj_ref[2 * C + i : 2 * C + i + 8, lanes])
                    * proj_ref[3 * C + i : 3 * C + i + 8, lanes]
                    * live
                )
                for tt in range(nt):
                    f_ref[(slot + tt) * C + i : (slot + tt) * C + i + 8, :] = left[:, tt * 128 : tt * 128 + 128]
                    row = (THIRD + slot + tt) * C + i
                    f_ref[row : row + 8, :] = right[:, tt * 128 : tt * 128 + 128]

        def pick(i):
            for k in range(8):
                c = i * 8 + k
                s_a[p, c] = jnp.concatenate(
                    [f_ref[pl.ds(c, 8, stride=C), :], f_ref[pl.ds(8 * C + c, 8, stride=C), :]], axis=0
                ).astype(BF)

        chunks(C // 8, pick)
        if p == 0:
            pl.semaphore_wait(entered, NQ - 1)
        exchange_start(s_a.at[p], r_a.at[p], by_channel, by_entry, sem_a.at[p])

    flip(gw_ref, gwt)
    flip(ow_ref, owt)
    flip(ti_ref, tit)
    for ref in (rf_ref, tin_acc, tout_acc, ow_acc, gw_acc, pw_acc, gn_acc):
        ref[...] = jnp.zeros_like(ref)
    for t0 in range(0, NT, THIRD):
        lanes = slice(t0 * 128, (t0 + THIRD) * 128)
        cott_ref[:, lanes] = load_t(cot_ref, t0, THIRD).astype(BF)
        gate_ref[:, lanes] = sigmoid(mm(gwt[...], scaled_ref[:, lanes]))

    for p in range(3):
        exchange_wait(s_a.at[p], r_a.at[p], sem_a.at[p])
        widen(r_a.at[p], fw_ref, p * ND * MSG)

        def per_col(qq):
            def tile(base, row0, stride):
                return lambda t: fw_ref[
                    pl.ds((t // THIRD) * ND * MSG + base * MSG + row0 + t % THIRD, 8, stride=stride), :
                ]

            rows = range(12 * p, 12 * p + 12)
            low = split_rows(tile(qq * NR, 0, MSG), rows)
            high = split_rows(tile(qq * NR + 8, 0, MSG), rows)
            for (ii, a), (_, b) in zip(low, high):
                put16(l_ref, ii, q_lanes(qq), a, b)
            for h in range(2):
                for jj, v in split_rows(tile(qq * NR + h, THIRD, 2 * MSG), rows):
                    rf_ref[pl.ds(qq * KP + h * TI + jj, 8, stride=128), :] = v
            if p == 2:
                r_ref[:, q_lanes(qq)] = rf_ref[pl.ds(pl.multiple_of(qq * KP, KP), KP), :].astype(BF)

        chunks(NQ, per_col)

    m_parts = ((0, A_ROWS, 0, 8, s_m0, r_m0), (A_ROWS, TI, 8, NT, s_m1, r_m1))
    for k, (i0, i1, t0, t1, src, dst) in enumerate(m_parts):
        rows = slice(i0 * NR, i1 * NR)
        size = src.shape[1]
        for b in range(0, KP, 256):
            c1_ref[rows, b : b + 256] = mm_nt(l_ref[rows, :], r_ref[b : b + 256, :])

        def pack(qq):
            for h in range(2):
                row = lambda ii: c1_ref[ii * NR + 8 * h : ii * NR + 8 * h + 8, q_lanes(qq)]
                for t, v in join_rows(row, range(t0, t1)):
                    f_ref[pl.ds((qq * NR + 8 * h) * size + t - t0, 8, stride=size), :] = v

        chunks(NQ, pack)
        narrow(f_ref, src)
        exchange_start(src, dst, by_entry, by_channel, sem_m.at[k])

    def middle(t0, nt, base, size, out0, out_size):
        w = nt * 128
        lanes = slice(t0 * 128, t0 * 128 + w)
        mixed = jnp.concatenate(
            [
                jnp.concatenate(
                    [fw_ref[pl.ds(base + tt + 8 * g * size, 8, stride=size), :] for g in range(C // 8)],
                    axis=0,
                )
                for tt in range(nt)
            ],
            axis=1,
        )
        normed_x, r_x = norm(mixed)
        scaled_out = (normed_x * gain_out()).astype(BF)
        output = mm(owt[...], scaled_out)
        gate = gate_ref[:, lanes]
        after = (xt_ref[:, lanes].astype(F32) + gate * output).astype(BF).astype(F32)
        normed_t, r_t = norm(after)
        scaled_t = (normed_t * gain_t()).astype(BF)
        cot_b = cott_ref[:, lanes]
        hid_ref[:, :w] = mm(tit[...], scaled_t)
        gi_ref[:, :w] = mm(to_ref[...], cot_b)
        for i in range(0, H, 16):
            g = hid_ref[i : i + 16, :w]
            u = hid_ref[H + i : H + i + 16, :w]
            gi = gi_ref[i : i + 16, :w]
            sg = sigmoid(g)
            swish = g * sg
            inner_ref[i : i + 16, :w] = (swish * u).astype(BF)
            gh_ref[i : i + 16, :w] = (gi * u * (sg + swish * (1.0 - sg))).astype(BF)
            gh_ref[H + i : H + i + 16, :w] = (gi * swish).astype(BF)
        back_t = mm(ti_ref[...], gh_ref[:, :w])
        tout_acc[...] += mm_nt(inner_ref[:, :w], cot_b)
        tin_acc[...] += mm_nt(gh_ref[:, :w], scaled_t)
        gn_acc[1] += fold(back_t * normed_t)
        grad_after = cot_b.astype(F32) + norm_back(back_t * gain_t(), normed_t, r_t)
        after_ref[:, lanes] = grad_after
        grad_output = (grad_after * gate).astype(BF)
        grad_logit = (grad_after * output * gate * (1.0 - gate)).astype(BF)
        logit_ref[:, lanes] = grad_logit
        gw_acc[...] += mm_nt(scaled_ref[:, lanes], grad_logit)
        ow_acc[...] += mm_nt(scaled_out, grad_output)
        back_x = mm(ow_ref[...], grad_output)
        gn_acc[0] += fold(back_x * normed_x)
        grad_mixed = norm_back(back_x * gain_out(), normed_x, r_x)
        for tt in range(nt):
            for g in range(C // 8):
                f_ref[pl.ds(out0 + tt + 8 * g * out_size, 8, stride=out_size), :] = grad_mixed[
                    8 * g : 8 * g + 8, tt * 128 : (tt + 1) * 128
                ]

    exchange_wait(s_m0, r_m0, sem_m.at[0])
    widen(r_m0, fw_ref)
    middle(0, 8, 0, 8, 0, MSG)
    exchange_wait(s_m1, r_m1, sem_m.at[1])
    widen(r_m1, fw_ref)
    middle(8, 5, 0, MSG, 8, MSG)
    narrow(f_ref, s_g0)
    exchange_start(s_g0, r_g0, by_channel, by_entry, sem_g.at[0])
    middle(G_TILES, 8, G_TILES - 8, MSG, 0, 8)
    narrow(f_ref, s_g1)
    exchange_start(s_g1, r_g1, by_channel, by_entry, sem_g.at[1])

    for p in range(3):
        exchange_wait_send(s_a.at[p], r_a.at[p], sem_a.at[p])
    s_b0, s_b1, r_b0, r_b1 = s_a.at[0], s_a.at[1], r_a.at[0], r_a.at[1]
    second = ND * MSG

    def operand(i0, i1):
        def per_col(qq):
            def tile(h):
                first = qq * NR + 8 * h

                def get(t):
                    if t < G_TILES:
                        return fw_ref[pl.ds(first * MSG + t, 8, stride=MSG), :]
                    return fw_ref[pl.ds(second + first * 8 + t - G_TILES, 8, stride=8), :]

                return get

            low, high = split_rows(tile(0), range(i0, i1)), split_rows(tile(1), range(i0, i1))
            for (ii, a), (_, b) in zip(low, high):
                put16(m_ref, ii, q_lanes(qq), a, b)

        chunks(NQ, per_col)
        rows = slice(i0 * NR, i1 * NR)
        for b in range(0, KP, 256):
            c1_ref[rows, b : b + 256] = mm(m_ref[rows, :], r_ref[:, b : b + 256])

    def pack_left(tiles, row0, size):
        def pack(qq):
            for h in range(2):
                row = lambda ii: c1_ref[ii * NR + 8 * h : ii * NR + 8 * h + 8, q_lanes(qq)]
                for t, v in join_rows(row, tiles):
                    f_ref[pl.ds((qq * NR + 8 * h) * size + row0 + t - tiles[0], 8, stride=size), :] = v

        chunks(NQ, pack)

    def pack_right(tiles, row0, size):
        def pack(qq):
            for h in range(2):
                row = lambda jj: rf_ref[pl.ds(qq * KP + h * TI + jj, 8, stride=128), :]
                for t, v in join_rows(row, tiles):
                    at = pl.ds((qq * NR + h) * size + row0 + t - tiles[0], 8, stride=2 * size)
                    f_ref[at, :] = v

        chunks(NQ, pack)

    exchange_wait(s_g0, r_g0, sem_g.at[0])
    widen(r_g0, fw_ref)
    operand(0, G_ROWS)
    pack_left(range(0, 12), 0, MSG)
    narrow(f_ref, s_b0)
    exchange_start(s_b0, r_b0, by_entry, by_channel, sem_b.at[0])

    core, chip = lax.rem(r, 2), (r // 2) * NQ + q
    sibling = r + 1 - 2 * core

    def put_terms(dst, first, value):
        half, at = divmod(first // MSG, HALF)
        n = value.shape[0] // MSG
        dst[half, at : at + n] = value.astype(BF).reshape(n, MSG, 128)

    def gain_rows(values):
        rows = [jnp.sum(v.T, axis=0, keepdims=True) for v in values]
        return jnp.concatenate(rows + [jnp.zeros((MSG - len(rows), 128), F32)], axis=0)

    put_terms(s_mid, 0, tin_acc[...])
    put_terms(s_mid, 2 * H, tout_acc[...])
    put_terms(s_mid, 3 * H, ow_acc[...])
    put_terms(s_mid, 3 * H + C, gw_acc[...])
    put_terms(s_mid, 3 * H + 2 * C, gain_rows([gn_acc[0], gn_acc[1]]))
    rest = (3 * H + 2 * C) // MSG - HALF + 1
    s_mid[1, rest:] = jnp.zeros((HALF - rest, MSG, 128), BF)

    def to_sibling(src, dst, sems):
        return pltpu.make_async_remote_copy(
            src_ref=src,
            dst_ref=dst,
            send_sem=sems.at[0],
            recv_sem=sems.at[1],
            device_id=(sibling, q),
            device_id_type=MESH,
        )

    def same_core(src, dst, sems, pick):
        cols = [lax.rem(q + d, NQ) for d in range(NQ)]

        def send(pr, pq):
            pltpu.make_async_remote_copy(
                src_ref=src.at[(pr // 2) * NQ + pq] if pick else src,
                dst_ref=dst.at[chip],
                send_sem=sems.at[0],
                recv_sem=sems.at[1],
                device_id=(pr, pq),
                device_id_type=MESH,
            ).start()

        for d in range(1, NQ):
            send(r, cols[d])

        def rows(k):
            for d in range(NQ):
                send(lax.rem(r + 2 * (k + 1), NR), cols[d])

        chunks(NR // 2 - 1, rows)
        pltpu.make_async_copy(src.at[chip] if pick else src, dst.at[chip], sems.at[2]).start()

    def along(axis, src, dst, sems, pick):
        n, at = (NR, r) if axis == "row" else (NQ, q)
        for d in range(1, n):
            peer = lax.rem(at + d, n)
            pltpu.make_async_remote_copy(
                src_ref=src.at[peer] if pick else src,
                dst_ref=dst.at[at],
                send_sem=sems.at[0],
                recv_sem=sems.at[1],
                device_id=(peer, q) if axis == "row" else (r, peer),
                device_id_type=MESH,
            ).start()
        pltpu.make_async_copy(src.at[at] if pick else src, dst.at[at], sems.at[2]).start()

    def along_wait(dst, sems):
        part = dst.at[pl.ds(0, dst.shape[0] - 1)]
        pltpu.make_async_copy(part, part, sems.at[1]).wait()
        pltpu.make_async_copy(dst.at[0], dst.at[0], sems.at[2]).wait()

    def along_wait_send(dst, sems):
        part = dst.at[pl.ds(0, dst.shape[0] - 1)]
        pltpu.make_async_copy(part, part, sems.at[0]).wait()

    to_sibling(s_mid.at[1 - core], h_mid, sem_mid.at[0]).start()

    to_sibling(s_mid.at[1 - core], h_mid, sem_mid.at[0]).wait()

    def pair_sum(i):
        at = pl.ds(i * 16, 16)
        p_mid[at] = (s_mid[core, at].astype(F32) + h_mid[at].astype(F32)).astype(BF)

    chunks(HALF // 16, pair_sum)
    same_core(p_mid, r_mid, sem_mid.at[1], True)
    exchange_wait(s_g1, r_g1, sem_g.at[1])
    widen(r_g1, fw_ref, second)
    operand(G_ROWS, TI)
    for b in range(0, KP, 128):
        mt_ref[b : b + 128, :] = mm_nt(eye(), m_ref[:, b : b + 128]).astype(BF)
    for b in range(0, KP, 256):
        both = mm(mt_ref[...], l_ref[:, b : b + 256])
        rf_ref[b // 128 * KP : (b // 128 + 1) * KP, :] = both[:, :128]
        rf_ref[(b // 128 + 1) * KP : (b // 128 + 2) * KP, :] = both[:, 128:]
    pack_left(range(12, NT), 0, MSG)
    pack_right(range(0, 7), 9, MSG)
    narrow(f_ref, s_b1)
    exchange_start(s_b1, r_b1, by_entry, by_channel, sem_b.at[1])
    pack_right(range(7, 15), 0, 8)
    narrow(f_ref, s_b2)
    exchange_start(s_b2, r_b2, by_entry, by_channel, sem_b.at[2])
    pack_right(range(15, NT), 0, 8)
    narrow(f_ref, s_b3)
    exchange_start(s_b3, r_b3, by_entry, by_channel, sem_b.at[3])

    along_wait(r_mid, sem_mid.at[1])
    add_blocks(r_mid, own_mid)
    same_core(own_mid, mid_sum.at[core], sem_mid.at[2], False)

    def left_at(t):
        return (t, MSG) if t < 12 else (second + t - 12, MSG)

    def right_at(t):
        if t < 7:
            return (second + 9 + t, MSG)
        return (2 * second + t - 7, 8) if t < 15 else (2 * second + ND * 8 + t - 15, 8)

    def project_back(t0, nt):
        w = nt * 128
        lanes = slice(t0 * 128, t0 * 128 + w)
        live = live_ref[0:1, lanes]
        for i in range(0, C, 16):
            for k, at in ((0, left_at), (2, right_at)):
                grad = []
                for t in range(t0, t0 + nt):
                    base, size = at(t)
                    grad.append(
                        jnp.concatenate(
                            [fw_ref[pl.ds(base + (i + 8 * g) * size, 8, stride=size), :] for g in range(2)],
                            axis=0,
                        )
                    )
                s = sigmoid(proj_ref[k * C + i : k * C + i + 16, lanes])
                gs = live * jnp.concatenate(grad, axis=1) * s
                gp_ref[(k + 1) * C + i : (k + 1) * C + i + 16, :w] = gs.astype(BF)
                gp_ref[k * C + i : k * C + i + 16, :w] = (
                    gs * proj_ref[(k + 1) * C + i : (k + 1) * C + i + 16, lanes] * (1.0 - s)
                ).astype(BF)
        normed, inverse = norm(xt_ref[:, lanes].astype(F32))
        pw_acc[...] += mm_nt(gp_ref[:, :w], scaled_ref[:, lanes])
        back = mm(pw_ref[...], gp_ref[:, :w]) + mm(gw_ref[...], logit_ref[:, lanes])
        gn_acc[2] += fold(back * normed)
        after_ref[:, lanes] += norm_back(back * gain_in(), normed, inverse)

    exchange_wait(s_b0, r_b0, sem_b.at[0])
    widen(r_b0, fw_ref)
    exchange_wait(s_b1, r_b1, sem_b.at[1])
    widen(r_b1, fw_ref, second)
    project_back(0, 7)
    exchange_wait(s_b2, r_b2, sem_b.at[2])
    widen(r_b2, fw_ref, 2 * second)
    project_back(7, 8)
    exchange_wait(s_b3, r_b3, sem_b.at[3])
    widen(r_b3, fw_ref, 2 * second + ND * 8)
    project_back(15, 6)

    own_rows = 4 * C // NR
    s_tail[:, 0:own_rows, :] = pw_acc[...].astype(BF).reshape(NR, own_rows, 128)
    last_gain = gain_rows([gn_acc[2]]).astype(BF)
    for k in range(NR):
        s_tail[k, own_rows : own_rows + MSG, :] = last_gain
    along("row", s_tail, r_tail, sem_tail.at[0], True)

    def pair_rows(t0):
        stop = min((t0 + 3) * 128, E)
        pair_o[t0 * 128 : stop, :] = after_ref[:, t0 * 128 : t0 * 128 + 384].T[: stop - t0 * 128].astype(BF)

    pair_rows(0)
    pair_rows(3)
    along_wait(r_tail, sem_tail.at[0])
    add_blocks(r_tail, row_tail)
    along("col", row_tail, q_tail, sem_tail.at[1], False)
    along_wait(mid_sum.at[core], sem_mid.at[2])
    to_sibling(mid_sum.at[core], mid_sum.at[core], sem_mid.at[3]).start()
    pair_rows(6)
    pair_rows(9)
    pair_rows(12)
    along_wait(q_tail, sem_tail.at[1])
    add_blocks(q_tail, all_tail)
    along("row", all_tail, tail_sum, sem_tail.at[2], False)
    pair_rows(15)
    pair_rows(18)
    to_sibling(mid_sum.at[core], mid_sum.at[core], sem_mid.at[3]).wait()
    along_wait(tail_sum, sem_tail.at[2])


    for k, (src, dst) in enumerate(((s_m0, r_m0), (s_m1, r_m1))):
        exchange_wait_send(src, dst, sem_m.at[k])
    for k, (src, dst) in enumerate(((s_g0, r_g0), (s_g1, r_g1))):
        exchange_wait_send(src, dst, sem_g.at[k])
    for k, (src, dst) in enumerate(((s_b0, r_b0), (s_b1, r_b1), (s_b2, r_b2), (s_b3, r_b3))):
        exchange_wait_send(src, dst, sem_b.at[k])
    along_wait_send(r_mid, sem_mid.at[1])
    along_wait_send(mid_sum.at[core], sem_mid.at[2])
    for k, dst in enumerate((r_tail, q_tail, tail_sum)):
        along_wait_send(dst, sem_tail.at[k])


def block(x, cot, live, pw, gw, ow, ti, to, gains):
    H = to.shape[0]
    wide = 1024
    tail = pw.shape[1] // NR + MSG
    msgs = lambda rows, *lead: pltpu.VMEM((*lead, ND, rows, 128), BF)
    dma = lambda *shape: pltpu.SemaphoreType.DMA(shape)
    v = pltpu.VMEM
    return pl.pallas_call(
        block_kernel,
        out_shape=(sds((E, C), BF), sds((2, HALF, MSG, 128), BF), sds((NR, tail, 128), BF)),
        in_specs=vspec(9),
        out_specs=tuple(vspec(3)),
        scratch_shapes=[
            v((4 * C, C), BF), v((C, C), BF), v((C, C), BF), v((2 * H, C), BF), v((C, C), F32),
            v((C, EP), BF), v((C, EP), BF), v((C, EP), BF), v((4 * C, EP), F32), v((C, EP), F32),
            v((C, EP), F32), v((C, EP), BF),
            v((ND * MSG, 128), F32), v((3 * ND * MSG, 128), F32),
            v((MROWS, KP), BF), v((KP, KP), BF), v((NQ * KP, 128), F32), v((MROWS, KP), BF),
            v((KP, MROWS), BF), v((MROWS, KP), F32),
            v((2 * H, wide), F32), v((H, wide), F32), v((H, wide), BF), v((2 * H, wide), BF),
            v((4 * C, wide), BF),
            v((2 * H, C), F32), v((H, C), F32), v((C, C), F32), v((C, C), F32), v((4 * C, C), F32),
            v((3, C, 128), F32),
            msgs(16, 3), msgs(16, 3), msgs(8), msgs(8), msgs(16), msgs(16), msgs(16), msgs(16),
            msgs(8), msgs(8), msgs(8), msgs(8), msgs(8), msgs(8),
            v((2, HALF, MSG, 128), BF), v((HALF, MSG, 128), BF), v((HALF, MSG, 128), BF),
            v((HALF, MSG, 128), BF), v((MSG, 128), BF),
            v((NR, tail, 128), BF), v((NR, tail, 128), BF), v((tail, 128), BF), v((NQ, tail, 128), BF),
            v((tail, 128), BF),
            dma(3, 3), dma(2, 3), dma(2, 3), dma(4, 3), dma(4, 3), dma(3, 3),
            pltpu.SemaphoreType.REGULAR,
        ],
        compiler_params=pltpu.CompilerParams(
            collective_id=1, has_side_effects=True, vmem_limit_bytes=VMEM_LIMIT
        ),
        name="block",
    )(x, cot, live, pw, gw, ow, ti, to, gains)


def finish_kernel(pair_ref, mid_ref, tail_ref, pair_o, pw_o, gw_o, ow_o, ti_o, to_o, gn_o):
    H = to_o.shape[0]
    scale = 1.0 / (TI * NR)

    def mid(first, rows):
        half, at = divmod(first // MSG, HALF)
        return mid_ref[half, at : at + rows // MSG].astype(F32).reshape(rows, 128) * scale

    pair_o[...] = pair_ref[...]
    for b in range(0, 2 * H, C):
        ti_o[:, b : b + C] = mid(b, C).T
    to_o[...] = mid(2 * H, H)
    ow_o[...] = mid(3 * H, C)
    gw_o[...] = mid(3 * H + C, C)
    own_rows = 4 * C // NR
    blocks = C // own_rows
    for b in range(4):
        pw = tail_ref[b * blocks : (b + 1) * blocks, 0:own_rows, :].astype(F32).reshape(C, 128)
        pw_o[:, b * C : (b + 1) * C] = pw.T * scale
    last_gain = tail_ref[0, own_rows : own_rows + MSG, :].astype(F32)[0:1] * scale
    gn_o[...] = jnp.concatenate([last_gain, mid(3 * H + 2 * C, MSG)[0:2]], axis=0)


def finish(pair, mid, tail, pw, gw, ow, ti, to, gains):
    return pl.pallas_call(
        finish_kernel,
        out_shape=(
            sds((E, C), BF), sds(pw.shape, F32), sds(gw.shape, F32), sds(ow.shape, F32),
            sds(ti.shape, F32), sds(to.shape, F32), sds(gains.shape, F32),
        ),
        in_specs=vspec(3),
        out_specs=tuple(vspec(7)),
        name="finish",
    )(pair, mid, tail)


def on_device(
    pair_act, cotangent, residue_mask, pair_mask, proj_weight, gate_weight, out_weight,
    trans_in, trans_out, norm_gains,
):
    live_res = residue_mask.astype(F32)
    row_live = lax.dynamic_slice_in_dim(live_res, lax.axis_index("row") * TI, TI)
    col_live = lax.dynamic_slice_in_dim(live_res, lax.axis_index("col") * TK, TK)
    live = pair_mask.astype(F32) * row_live[:, None] * col_live[None, :]
    live = jnp.pad(live.reshape(1, E), ((0, 7), (0, EP - E)))
    weights = (proj_weight, gate_weight, out_weight, trans_in, trans_out, norm_gains)
    sums = block(pair_act.reshape(E, C), cotangent.reshape(E, C), live, *weights)
    out = finish(*sums, *weights)
    return (out[0].reshape(TI, TK, C), *out[1:])


def solution(mesh):
    split = P("row", "col", None)
    in_specs = (split, split, P(), P("row", "col"), P(), P(), P(), P(), P(), P())
    out_specs = (split, P(), P(), P(), P(), P(), P())
    return jax.shard_map(
        on_device, mesh=mesh, in_specs=in_specs, out_specs=out_specs, check_vma=False
    )
```

```python
import functools

import jax
import jax.numpy as jnp
from jax import lax
from jax.experimental import pallas as pl
from jax.experimental.pallas import tpu as pltpu
from jax.sharding import PartitionSpec as P

EPSILON = 1e-05
BF = jnp.bfloat16
F32 = jnp.float32
MESH = pl.DeviceIdType.MESH
C = 128
NR, NQ = 16, 8
ND = NR * NQ
TI, TK = 36, 72
E = TI * TK
NT = 21
EP = NT * 128
MROWS = TI * NR
KP = NQ * 128
MSG = 16
HALF = ND // 2
M_ROWS = 16, 29
G_ROWS = 14, 28
AHEAD = 15
THIRD = 7
VMEM_LIMIT = 60 * 2**20


def vspec(n):
    return [pl.BlockSpec(memory_space=pltpu.VMEM)] * n


def sds(shape, dtype):
    return jax.ShapeDtypeStruct(shape, dtype)


def sigmoid(v):
    return 0.5 * jnp.tanh(0.5 * v) + 0.5


def norm(v):
    center = v - jnp.mean(v, axis=0, keepdims=True)
    inverse = lax.rsqrt(jnp.mean(center * center, axis=0, keepdims=True) + EPSILON)
    return center * inverse, inverse


def norm_back(h, n, inverse):
    first = jnp.mean(h, axis=0, keepdims=True)
    second = jnp.mean(h * n, axis=0, keepdims=True)
    return inverse * (h - first - n * second)


def mm(a, b):
    return jnp.dot(a, b, preferred_element_type=F32)


def mm_nt(a, b):
    return lax.dot_general(a, b, (((1,), (1,)), ((), ())), preferred_element_type=F32)


def eye():
    return (
        lax.broadcasted_iota(jnp.int32, (C, C), 0) == lax.broadcasted_iota(jnp.int32, (C, C), 1)
    ).astype(BF)


def each_peer(fn):
    r, q = lax.axis_index("row"), lax.axis_index("col")

    cols = [lax.rem(q + dq, NQ) for dq in range(NQ)]

    def one(pr, dq):
        fn(pr, cols[dq])

    for dq in range(1, NQ):
        one(r, dq)

    def body(dr, carry):
        pr = lax.rem(r + dr, NR)
        for dq in range(NQ):
            one(pr, dq)
        return carry

    lax.fori_loop(1, NR, body, 0)


def exchange_start(src, dst, src_slot, dst_slot, sems):
    r, q = lax.axis_index("row"), lax.axis_index("col")
    mine = dst_slot(r, q)

    def send(pr, pq):
        pltpu.make_async_remote_copy(
            src_ref=src.at[src_slot(pr, pq)],
            dst_ref=dst.at[mine],
            send_sem=sems.at[0],
            recv_sem=sems.at[1],
            device_id=(pr, pq),
            device_id_type=MESH,
        ).start()

    each_peer(send)
    pltpu.make_async_copy(src.at[src_slot(r, q)], dst.at[mine], sems.at[2]).start()


def exchange_wait(src, dst, sems):
    part = pl.ds(0, ND - 1)
    pltpu.make_async_copy(src.at[part], dst.at[part], sems.at[1]).wait()
    pltpu.make_async_copy(src.at[0], dst.at[0], sems.at[2]).wait()


def exchange_wait_send(src, dst, sems):
    part = pl.ds(0, ND - 1)
    pltpu.make_async_copy(src.at[part], dst.at[part], sems.at[0]).wait()


def by_channel(r, q):
    return r * NQ + q


def by_entry(r, q):
    return q * NR + r


def chunks(count, fn):
    def loop(i, carry):
        fn(i)
        return carry

    lax.fori_loop(0, count, loop, 0)


def widen(src, f_ref, base=0):
    rows = src.shape[1]

    def some(i):
        f_ref[pl.ds(pl.multiple_of(base + i * 16 * rows, 128), 16 * rows), :] = (
            src[pl.ds(i * 16, 16)].astype(F32).reshape(16 * rows, 128)
        )

    chunks(ND // 16, some)


def narrow(f_ref, dst):
    rows = dst.shape[1]

    def some(i):
        dst[pl.ds(i * 16, 16)] = (
            f_ref[pl.ds(pl.multiple_of(i * 16 * rows, 128), 16 * rows), :].reshape(16, rows, 128).astype(BF)
        )

    chunks(ND // 16, some)


def lane_iota():
    return lax.broadcasted_iota(jnp.int32, (8, 128), 1)


def roll(v, shift):
    shift %= 128
    return v if shift == 0 else pltpu.roll(v, shift, 1)


def split_rows(tile, rows):
    lane = lane_iota()
    tiles = {}

    def get(t):
        if t not in tiles:
            tiles[t] = tile(t)
        return tiles[t]

    out = []
    for ii in rows:
        t, l = divmod(TK * ii, 128)
        v = get(t)
        if l + TK > 128:
            v = jnp.where(lane >= l, v, get(t + 1))
        out.append((ii, jnp.where(lane < TK, roll(v, -l), 0.0)))
    return out


def join_rows(row, tiles):
    lane = lane_iota()
    rolled = {}
    out = []
    for t in tiles:
        first = (128 * t) // TK
        final = min((128 * t + 127) // TK, TI - 1)
        value = jnp.zeros((8, 128), F32)
        for ii in range(final, first - 1, -1):
            start = TK * ii - 128 * t
            if ii not in rolled:
                rolled[ii] = roll(row(ii), start)
            if ii == final and start + TK >= 128:
                value = rolled[ii]
            else:
                value = jnp.where(lane < start + TK, rolled[ii], value)
        out.append((t, value))
    return out


def put16(ref, ii, lanes, low, high):
    ref[ii * NR : (ii + 1) * NR, lanes] = jnp.concatenate([low, high], axis=0).astype(BF)


def q_lanes(q):
    return pl.ds(pl.multiple_of(q * 128, 128), 128)


def fold(v):
    return sum(v[:, k : k + 128] for k in range(128, v.shape[1], 128)) + v[:, :128]


def add_blocks(ref, dst):
    total = ref[0].astype(F32)
    for k in range(1, ref.shape[0]):
        total = total + ref[k].astype(F32)
    dst[...] = total.astype(BF)


def block_kernel(
    x_ref, cot_ref, live_ref, pw_ref, gw_ref, ow_ref, ti_ref, to_ref, gain_ref,
    pair_o, mid_sum, tail_sum,
    pwt, gwt, owt, tit, gcol, xt_ref, cott_ref, scaled_ref, proj_ref, gate_ref,
    after_ref, logit_ref, f_ref, fw_ref, l_ref, r_ref, rf_ref, m_ref, mt_ref, c1_ref,
    hid_ref, gi_ref, inner_ref, gh_ref, gp_ref, tin_acc, tout_acc, ow_acc, gw_acc, pw_acc, gn_acc,
    s_a, r_a, s_m0, r_m0, s_m1, r_m1, s_m2, r_m2, s_g0, r_g0, s_g1, r_g1, s_g2, r_g2,
    s_b2, r_b2, s_b3, r_b3,
    s_mid, h_mid, p_mid, r_mid, own_mid,
    s_tail, r_tail, row_tail, q_tail, all_tail,
    sem_a, sem_m, sem_g, sem_b, sem_mid, sem_tail, entered,
):
    H = to_ref.shape[0]
    r, q = lax.axis_index("row"), lax.axis_index("col")
    me = by_channel(r, q)

    barrier = pltpu.get_barrier_semaphore()

    def greet(sem, pr, pq):
        pl.semaphore_signal(sem, inc=1, device_id=(pr, pq), device_id_type=MESH)

    for d in range(1, NQ):
        greet(barrier, r, lax.rem(q + d, NQ))
    for d in range(1, NR):
        greet(barrier, lax.rem(r + d, NR), q)

    def flip(src, dst):
        for b in range(src.shape[1] // C):
            dst[b * C : (b + 1) * C, :] = src[:, b * C : (b + 1) * C].astype(F32).T.astype(BF)

    flip(pw_ref, pwt)
    gcol[...] = jnp.concatenate([gain_ref[...], jnp.zeros((C - 3, C), F32)], axis=0).T
    gain_in, gain_out, gain_t = (lambda: gcol[:, 0:1]), (lambda: gcol[:, 1:2]), (lambda: gcol[:, 2:3])

    def load_t(ref, t0, nt):
        stop = min((t0 + nt) * 128, E)
        rows = ref[t0 * 128 : stop, :]
        pad = (t0 + nt) * 128 - stop
        if pad:
            rows = jnp.concatenate([rows, jnp.zeros((pad, C), rows.dtype)], axis=0)
        return mm_nt(eye(), rows)

    pl.semaphore_wait(barrier, NR + NQ - 2)
    for d in range(1, NQ):
        greet(entered, r, lax.rem(q + d, NQ))

    f_ref[2 * THIRD * C :, :] = jnp.zeros(((MSG - 2 * THIRD) * C, 128), F32)
    for p in range(3):
        for t0, slot, nt in ((p * THIRD, 0, THIRD),):
            lanes = slice(t0 * 128, (t0 + nt) * 128)
            xt = load_t(x_ref, t0, nt)
            xt_ref[:, lanes] = xt.astype(BF)
            scaled = (norm(xt)[0] * gain_in()).astype(BF)
            scaled_ref[:, lanes] = scaled
            proj_ref[:, lanes] = mm(pwt[...], scaled)
            live = live_ref[0:1, lanes]
            for i in range(0, C, 8):
                left = sigmoid(proj_ref[i : i + 8, lanes]) * proj_ref[C + i : C + i + 8, lanes] * live
                right = (
                    sigmoid(proj_ref[2 * C + i : 2 * C + i + 8, lanes])
                    * proj_ref[3 * C + i : 3 * C + i + 8, lanes]
                    * live
                )
                for tt in range(nt):
                    f_ref[(slot + tt) * C + i : (slot + tt) * C + i + 8, :] = left[:, tt * 128 : tt * 128 + 128]
                    row = (THIRD + slot + tt) * C + i
                    f_ref[row : row + 8, :] = right[:, tt * 128 : tt * 128 + 128]

        def pick(i):
            for k in range(8):
                c = i * 8 + k
                s_a[p, c] = jnp.concatenate(
                    [f_ref[pl.ds(c, 8, stride=C), :], f_ref[pl.ds(8 * C + c, 8, stride=C), :]], axis=0
                ).astype(BF)

        chunks(C // 8, pick)
        if p == 0:
            pl.semaphore_wait(entered, NQ - 1)
        exchange_start(s_a.at[p], r_a.at[p], by_channel, by_entry, sem_a.at[p])

    flip(gw_ref, gwt)
    flip(ow_ref, owt)
    flip(ti_ref, tit)
    for ref in (rf_ref, tin_acc, tout_acc, ow_acc, gw_acc, pw_acc, gn_acc):
        ref[...] = jnp.zeros_like(ref)
    for t0 in range(0, NT, THIRD):
        lanes = slice(t0 * 128, (t0 + THIRD) * 128)
        cott_ref[:, lanes] = load_t(cot_ref, t0, THIRD).astype(BF)
        gate_ref[:, lanes] = sigmoid(mm(gwt[...], scaled_ref[:, lanes]))

    for p in range(3):
        exchange_wait(s_a.at[p], r_a.at[p], sem_a.at[p])
        widen(r_a.at[p], fw_ref, p * ND * MSG)

        def per_col(qq):
            def tile(base, row0, stride):
                return lambda t: fw_ref[
                    pl.ds((t // THIRD) * ND * MSG + base * MSG + row0 + t % THIRD, 8, stride=stride), :
                ]

            rows = range(12 * p, 12 * p + 12)
            low = split_rows(tile(qq * NR, 0, MSG), rows)
            high = split_rows(tile(qq * NR + 8, 0, MSG), rows)
            for (ii, a), (_, b) in zip(low, high):
                put16(l_ref, ii, q_lanes(qq), a, b)
            for h in range(2):
                for jj, v in split_rows(tile(qq * NR + h, THIRD, 2 * MSG), rows):
                    rf_ref[pl.ds(qq * KP + h * TI + jj, 8, stride=128), :] = v
            if p == 2:
                r_ref[:, q_lanes(qq)] = rf_ref[pl.ds(pl.multiple_of(qq * KP, KP), KP), :].astype(BF)

        chunks(NQ, per_col)

    m_parts = (
        (0, M_ROWS[0], 0, 8, s_m0, r_m0),
        (M_ROWS[0], M_ROWS[1], 8, 16, s_m1, r_m1),
        (M_ROWS[1], TI, 16, NT, s_m2, r_m2),
    )
    for k, (i0, i1, t0, t1, src, dst) in enumerate(m_parts):
        rows = slice(i0 * NR, i1 * NR)
        size = src.shape[1]
        for b in range(0, KP, 256):
            c1_ref[rows, b : b + 256] = mm_nt(l_ref[rows, :], r_ref[b : b + 256, :])

        def pack(qq):
            for h in range(2):
                row = lambda ii: c1_ref[ii * NR + 8 * h : ii * NR + 8 * h + 8, q_lanes(qq)]
                for t, v in join_rows(row, range(t0, t1)):
                    f_ref[pl.ds((qq * NR + 8 * h) * size + t - t0, 8, stride=size), :] = v

        chunks(NQ, pack)
        narrow(f_ref, src)
        exchange_start(src, dst, by_entry, by_channel, sem_m.at[k])

    def middle(t0, nt, base, size, out0, out_size):
        w = nt * 128
        lanes = slice(t0 * 128, t0 * 128 + w)
        mixed = jnp.concatenate(
            [
                jnp.concatenate(
                    [fw_ref[pl.ds(base + tt + 8 * g * size, 8, stride=size), :] for g in range(C // 8)],
                    axis=0,
                )
                for tt in range(nt)
            ],
            axis=1,
        )
        normed_x, r_x = norm(mixed)
        scaled_out = (normed_x * gain_out()).astype(BF)
        output = mm(owt[...], scaled_out)
        gate = gate_ref[:, lanes]
        after = (xt_ref[:, lanes].astype(F32) + gate * output).astype(BF).astype(F32)
        normed_t, r_t = norm(after)
        scaled_t = (normed_t * gain_t()).astype(BF)
        cot_b = cott_ref[:, lanes]
        hid_ref[:, :w] = mm(tit[...], scaled_t)
        gi_ref[:, :w] = mm(to_ref[...], cot_b)
        for i in range(0, H, 16):
            g = hid_ref[i : i + 16, :w]
            u = hid_ref[H + i : H + i + 16, :w]
            gi = gi_ref[i : i + 16, :w]
            sg = sigmoid(g)
            swish = g * sg
            inner_ref[i : i + 16, :w] = (swish * u).astype(BF)
            gh_ref[i : i + 16, :w] = (gi * u * (sg + swish * (1.0 - sg))).astype(BF)
            gh_ref[H + i : H + i + 16, :w] = (gi * swish).astype(BF)
        back_t = mm(ti_ref[...], gh_ref[:, :w])
        tout_acc[...] += mm_nt(inner_ref[:, :w], cot_b)
        tin_acc[...] += mm_nt(gh_ref[:, :w], scaled_t)
        gn_acc[1] += fold(back_t * normed_t)
        grad_after = cot_b.astype(F32) + norm_back(back_t * gain_t(), normed_t, r_t)
        after_ref[:, lanes] = grad_after
        grad_output = (grad_after * gate).astype(BF)
        grad_logit = (grad_after * output * gate * (1.0 - gate)).astype(BF)
        logit_ref[:, lanes] = grad_logit
        gw_acc[...] += mm_nt(scaled_ref[:, lanes], grad_logit)
        ow_acc[...] += mm_nt(scaled_out, grad_output)
        back_x = mm(ow_ref[...], grad_output)
        gn_acc[0] += fold(back_x * normed_x)
        grad_mixed = norm_back(back_x * gain_out(), normed_x, r_x)
        for tt in range(nt):
            for g in range(C // 8):
                f_ref[pl.ds(out0 + tt + 8 * g * out_size, 8, stride=out_size), :] = grad_mixed[
                    8 * g : 8 * g + 8, tt * 128 : (tt + 1) * 128
                ]

    third = ND * 8
    g_parts = ((s_g0, r_g0), (s_g1, r_g1), (s_g2, r_g2))
    for k, (_, _, t0, t1, src, dst) in enumerate(m_parts):
        exchange_wait(src, dst, sem_m.at[k])
        widen(dst, fw_ref, k * third)
        middle(t0, t1 - t0, k * third, 8, 0, 8)
        narrow(f_ref, g_parts[k][0])
        exchange_start(*g_parts[k], by_channel, by_entry, sem_g.at[k])

    for p in range(3):
        exchange_wait_send(s_a.at[p], r_a.at[p], sem_a.at[p])
    s_b0, s_b1, r_b0, r_b1 = s_a.at[0], s_a.at[1], r_a.at[0], r_a.at[1]
    second = ND * MSG

    def operand(i0, i1):
        def per_col(qq):
            def tile(h):
                first = qq * NR + 8 * h

                def get(t):
                    return fw_ref[pl.ds((t // 8) * third + first * 8 + t % 8, 8, stride=8), :]

                return get

            low, high = split_rows(tile(0), range(i0, i1)), split_rows(tile(1), range(i0, i1))
            for (ii, a), (_, b) in zip(low, high):
                put16(m_ref, ii, q_lanes(qq), a, b)

        chunks(NQ, per_col)
        rows = slice(i0 * NR, i1 * NR)
        for b in range(0, KP, 256):
            c1_ref[rows, b : b + 256] = mm(m_ref[rows, :], r_ref[:, b : b + 256])

    def pack_left(tiles, row0, size):
        def pack(qq):
            for h in range(2):
                row = lambda ii: c1_ref[ii * NR + 8 * h : ii * NR + 8 * h + 8, q_lanes(qq)]
                for t, v in join_rows(row, tiles):
                    f_ref[pl.ds((qq * NR + 8 * h) * size + row0 + t - tiles[0], 8, stride=size), :] = v

        chunks(NQ, pack)

    def pack_right(tiles, row0, size):
        def pack(qq):
            for h in range(2):
                row = lambda jj: rf_ref[pl.ds(qq * KP + h * TI + jj, 8, stride=128), :]
                for t, v in join_rows(row, tiles):
                    at = pl.ds((qq * NR + h) * size + row0 + t - tiles[0], 8, stride=2 * size)
                    f_ref[at, :] = v

        chunks(NQ, pack)

    exchange_wait(s_g0, r_g0, sem_g.at[0])
    widen(r_g0, fw_ref)
    operand(0, G_ROWS[0])
    exchange_wait(s_g1, r_g1, sem_g.at[1])
    widen(r_g1, fw_ref, third)
    operand(G_ROWS[0], G_ROWS[1])
    pack_left(range(0, AHEAD), 0, MSG)
    narrow(f_ref, s_b0)
    exchange_start(s_b0, r_b0, by_entry, by_channel, sem_b.at[0])

    core, chip = lax.rem(r, 2), (r // 2) * NQ + q
    sibling = r + 1 - 2 * core

    def put_terms(dst, first, value):
        half, at = divmod(first // MSG, HALF)
        n = value.shape[0] // MSG
        dst[half, at : at + n] = value.astype(BF).reshape(n, MSG, 128)

    def gain_rows(values):
        rows = [jnp.sum(v.T, axis=0, keepdims=True) for v in values]
        return jnp.concatenate(rows + [jnp.zeros((MSG - len(rows), 128), F32)], axis=0)

    put_terms(s_mid, 0, tin_acc[...])
    put_terms(s_mid, 2 * H, tout_acc[...])
    put_terms(s_mid, 3 * H, ow_acc[...])
    put_terms(s_mid, 3 * H + C, gw_acc[...])
    put_terms(s_mid, 3 * H + 2 * C, gain_rows([gn_acc[0], gn_acc[1]]))
    rest = (3 * H + 2 * C) // MSG - HALF + 1
    s_mid[1, rest:] = jnp.zeros((HALF - rest, MSG, 128), BF)

    def to_sibling(src, dst, sems):
        return pltpu.make_async_remote_copy(
            src_ref=src,
            dst_ref=dst,
            send_sem=sems.at[0],
            recv_sem=sems.at[1],
            device_id=(sibling, q),
            device_id_type=MESH,
        )

    def same_core(src, dst, sems, pick):
        cols = [lax.rem(q + d, NQ) for d in range(NQ)]

        def send(pr, pq):
            pltpu.make_async_remote_copy(
                src_ref=src.at[(pr // 2) * NQ + pq] if pick else src,
                dst_ref=dst.at[chip],
                send_sem=sems.at[0],
                recv_sem=sems.at[1],
                device_id=(pr, pq),
                device_id_type=MESH,
            ).start()

        for d in range(1, NQ):
            send(r, cols[d])

        def rows(k):
            for d in range(NQ):
                send(lax.rem(r + 2 * (k + 1), NR), cols[d])

        chunks(NR // 2 - 1, rows)
        pltpu.make_async_copy(src.at[chip] if pick else src, dst.at[chip], sems.at[2]).start()

    def along(axis, src, dst, sems, pick):
        n, at = (NR, r) if axis == "row" else (NQ, q)
        for d in range(1, n):
            peer = lax.rem(at + d, n)
            pltpu.make_async_remote_copy(
                src_ref=src.at[peer] if pick else src,
                dst_ref=dst.at[at],
                send_sem=sems.at[0],
                recv_sem=sems.at[1],
                device_id=(peer, q) if axis == "row" else (r, peer),
                device_id_type=MESH,
            ).start()
        pltpu.make_async_copy(src.at[at] if pick else src, dst.at[at], sems.at[2]).start()

    def along_wait(dst, sems):
        part = dst.at[pl.ds(0, dst.shape[0] - 1)]
        pltpu.make_async_copy(part, part, sems.at[1]).wait()
        pltpu.make_async_copy(dst.at[0], dst.at[0], sems.at[2]).wait()

    def along_wait_send(dst, sems):
        part = dst.at[pl.ds(0, dst.shape[0] - 1)]
        pltpu.make_async_copy(part, part, sems.at[0]).wait()

    to_sibling(s_mid.at[1 - core], h_mid, sem_mid.at[0]).start()

    to_sibling(s_mid.at[1 - core], h_mid, sem_mid.at[0]).wait()

    def pair_sum(i):
        at = pl.ds(i * 16, 16)
        p_mid[at] = (s_mid[core, at].astype(F32) + h_mid[at].astype(F32)).astype(BF)

    chunks(HALF // 16, pair_sum)
    same_core(p_mid, r_mid, sem_mid.at[1], True)
    exchange_wait(s_g2, r_g2, sem_g.at[2])
    widen(r_g2, fw_ref, 2 * third)
    operand(G_ROWS[1], TI)
    for b in range(0, KP, 128):
        mt_ref[b : b + 128, :] = mm_nt(eye(), m_ref[:, b : b + 128]).astype(BF)
    for b in range(0, KP, 256):
        both = mm(mt_ref[...], l_ref[:, b : b + 256])
        rf_ref[b // 128 * KP : (b // 128 + 1) * KP, :] = both[:, :128]
        rf_ref[(b // 128 + 1) * KP : (b // 128 + 2) * KP, :] = both[:, 128:]
    pack_left(range(AHEAD, NT), 0, MSG)
    pack_right(range(0, 10), NT - AHEAD, MSG)
    narrow(f_ref, s_b1)
    exchange_start(s_b1, r_b1, by_entry, by_channel, sem_b.at[1])
    pack_right(range(10, 18), 0, 8)
    narrow(f_ref, s_b2)
    exchange_start(s_b2, r_b2, by_entry, by_channel, sem_b.at[2])
    pack_right(range(18, NT), 0, 8)
    narrow(f_ref, s_b3)
    exchange_start(s_b3, r_b3, by_entry, by_channel, sem_b.at[3])

    along_wait(r_mid, sem_mid.at[1])
    add_blocks(r_mid, own_mid)
    same_core(own_mid, mid_sum.at[core], sem_mid.at[2], False)

    def left_at(t):
        return (t, MSG) if t < AHEAD else (second + t - AHEAD, MSG)

    def right_at(t):
        if t < 10:
            return (second + NT - AHEAD + t, MSG)
        return (2 * second + t - 10, 8) if t < 18 else (2 * second + third + t - 18, 8)

    def project_back(t0, nt):
        w = nt * 128
        lanes = slice(t0 * 128, t0 * 128 + w)
        live = live_ref[0:1, lanes]
        for i in range(0, C, 16):
            for k, at in ((0, left_at), (2, right_at)):
                grad = []
                for t in range(t0, t0 + nt):
                    base, size = at(t)
                    grad.append(
                        jnp.concatenate(
                            [fw_ref[pl.ds(base + (i + 8 * g) * size, 8, stride=size), :] for g in range(2)],
                            axis=0,
                        )
                    )
                s = sigmoid(proj_ref[k * C + i : k * C + i + 16, lanes])
                gs = live * jnp.concatenate(grad, axis=1) * s
                gp_ref[(k + 1) * C + i : (k + 1) * C + i + 16, :w] = gs.astype(BF)
                gp_ref[k * C + i : k * C + i + 16, :w] = (
                    gs * proj_ref[(k + 1) * C + i : (k + 1) * C + i + 16, lanes] * (1.0 - s)
                ).astype(BF)
        normed, inverse = norm(xt_ref[:, lanes].astype(F32))
        pw_acc[...] += mm_nt(gp_ref[:, :w], scaled_ref[:, lanes])
        back = mm(pw_ref[...], gp_ref[:, :w]) + mm(gw_ref[...], logit_ref[:, lanes])
        gn_acc[2] += fold(back * normed)
        after_ref[:, lanes] += norm_back(back * gain_in(), normed, inverse)

    exchange_wait(s_b0, r_b0, sem_b.at[0])
    widen(r_b0, fw_ref)
    exchange_wait(s_b1, r_b1, sem_b.at[1])
    widen(r_b1, fw_ref, second)
    project_back(0, 8)
    exchange_wait(s_b2, r_b2, sem_b.at[2])
    widen(r_b2, fw_ref, 2 * second)
    project_back(8, 8)
    exchange_wait(s_b3, r_b3, sem_b.at[3])
    widen(r_b3, fw_ref, 2 * second + ND * 8)
    project_back(16, 5)

    own_rows = 4 * C // NR
    s_tail[:, 0:own_rows, :] = pw_acc[...].astype(BF).reshape(NR, own_rows, 128)
    last_gain = gain_rows([gn_acc[2]]).astype(BF)
    for k in range(NR):
        s_tail[k, own_rows : own_rows + MSG, :] = last_gain
    along("row", s_tail, r_tail, sem_tail.at[0], True)

    def pair_rows(t0):
        stop = min((t0 + 3) * 128, E)
        pair_o[t0 * 128 : stop, :] = after_ref[:, t0 * 128 : t0 * 128 + 384].T[: stop - t0 * 128].astype(BF)

    pair_rows(0)
    pair_rows(3)
    along_wait(r_tail, sem_tail.at[0])
    add_blocks(r_tail, row_tail)
    along("col", row_tail, q_tail, sem_tail.at[1], False)
    along_wait(mid_sum.at[core], sem_mid.at[2])
    to_sibling(mid_sum.at[core], mid_sum.at[core], sem_mid.at[3]).start()
    pair_rows(6)
    pair_rows(9)
    pair_rows(12)
    along_wait(q_tail, sem_tail.at[1])
    add_blocks(q_tail, all_tail)
    along("row", all_tail, tail_sum, sem_tail.at[2], False)
    pair_rows(15)
    pair_rows(18)
    to_sibling(mid_sum.at[core], mid_sum.at[core], sem_mid.at[3]).wait()
    along_wait(tail_sum, sem_tail.at[2])


    for k, (_, _, _, _, src, dst) in enumerate(m_parts):
        exchange_wait_send(src, dst, sem_m.at[k])
    for k, (src, dst) in enumerate(g_parts):
        exchange_wait_send(src, dst, sem_g.at[k])
    for k, (src, dst) in enumerate(((s_b0, r_b0), (s_b1, r_b1), (s_b2, r_b2), (s_b3, r_b3))):
        exchange_wait_send(src, dst, sem_b.at[k])
    along_wait_send(r_mid, sem_mid.at[1])
    along_wait_send(mid_sum.at[core], sem_mid.at[2])
    for k, dst in enumerate((r_tail, q_tail, tail_sum)):
        along_wait_send(dst, sem_tail.at[k])


def block(x, cot, live, pw, gw, ow, ti, to, gains):
    H = to.shape[0]
    wide = 1024
    tail = pw.shape[1] // NR + MSG
    msgs = lambda rows, *lead: pltpu.VMEM((*lead, ND, rows, 128), BF)
    dma = lambda *shape: pltpu.SemaphoreType.DMA(shape)
    v = pltpu.VMEM
    return pl.pallas_call(
        block_kernel,
        out_shape=(sds((E, C), BF), sds((2, HALF, MSG, 128), BF), sds((NR, tail, 128), BF)),
        in_specs=vspec(9),
        out_specs=tuple(vspec(3)),
        scratch_shapes=[
            v((4 * C, C), BF), v((C, C), BF), v((C, C), BF), v((2 * H, C), BF), v((C, C), F32),
            v((C, EP), BF), v((C, EP), BF), v((C, EP), BF), v((4 * C, EP), F32), v((C, EP), F32),
            v((C, EP), F32), v((C, EP), BF),
            v((ND * MSG, 128), F32), v((3 * ND * MSG, 128), F32),
            v((MROWS, KP), BF), v((KP, KP), BF), v((NQ * KP, 128), F32), v((MROWS, KP), BF),
            v((KP, MROWS), BF), v((MROWS, KP), F32),
            v((2 * H, wide), F32), v((H, wide), F32), v((H, wide), BF), v((2 * H, wide), BF),
            v((4 * C, wide), BF),
            v((2 * H, C), F32), v((H, C), F32), v((C, C), F32), v((C, C), F32), v((4 * C, C), F32),
            v((3, C, 128), F32),
            msgs(16, 3), msgs(16, 3), *[msgs(8)] * 16,
            v((2, HALF, MSG, 128), BF), v((HALF, MSG, 128), BF), v((HALF, MSG, 128), BF),
            v((HALF, MSG, 128), BF), v((MSG, 128), BF),
            v((NR, tail, 128), BF), v((NR, tail, 128), BF), v((tail, 128), BF), v((NQ, tail, 128), BF),
            v((tail, 128), BF),
            dma(3, 3), dma(3, 3), dma(3, 3), dma(4, 3), dma(4, 3), dma(3, 3),
            pltpu.SemaphoreType.REGULAR,
        ],
        compiler_params=pltpu.CompilerParams(
            collective_id=1, has_side_effects=True, vmem_limit_bytes=VMEM_LIMIT
        ),
        name="block",
    )(x, cot, live, pw, gw, ow, ti, to, gains)


def finish_kernel(pair_ref, mid_ref, tail_ref, pair_o, pw_o, gw_o, ow_o, ti_o, to_o, gn_o):
    H = to_o.shape[0]
    scale = 1.0 / (TI * NR)

    def mid(first, rows):
        half, at = divmod(first // MSG, HALF)
        return mid_ref[half, at : at + rows // MSG].astype(F32).reshape(rows, 128) * scale

    pair_o[...] = pair_ref[...]
    for b in range(0, 2 * H, C):
        ti_o[:, b : b + C] = mid(b, C).T
    to_o[...] = mid(2 * H, H)
    ow_o[...] = mid(3 * H, C)
    gw_o[...] = mid(3 * H + C, C)
    own_rows = 4 * C // NR
    blocks = C // own_rows
    for b in range(4):
        pw = tail_ref[b * blocks : (b + 1) * blocks, 0:own_rows, :].astype(F32).reshape(C, 128)
        pw_o[:, b * C : (b + 1) * C] = pw.T * scale
    last_gain = tail_ref[0, own_rows : own_rows + MSG, :].astype(F32)[0:1] * scale
    gn_o[...] = jnp.concatenate([last_gain, mid(3 * H + 2 * C, MSG)[0:2]], axis=0)


def finish(pair, mid, tail, pw, gw, ow, ti, to, gains):
    return pl.pallas_call(
        finish_kernel,
        out_shape=(
            sds((E, C), BF), sds(pw.shape, F32), sds(gw.shape, F32), sds(ow.shape, F32),
            sds(ti.shape, F32), sds(to.shape, F32), sds(gains.shape, F32),
        ),
        in_specs=vspec(3),
        out_specs=tuple(vspec(7)),
        name="finish",
    )(pair, mid, tail)


def on_device(
    pair_act, cotangent, residue_mask, pair_mask, proj_weight, gate_weight, out_weight,
    trans_in, trans_out, norm_gains,
):
    live_res = residue_mask.astype(F32)
    row_live = lax.dynamic_slice_in_dim(live_res, lax.axis_index("row") * TI, TI)
    col_live = lax.dynamic_slice_in_dim(live_res, lax.axis_index("col") * TK, TK)
    live = pair_mask.astype(F32) * row_live[:, None] * col_live[None, :]
    live = jnp.pad(live.reshape(1, E), ((0, 7), (0, EP - E)))
    weights = (proj_weight, gate_weight, out_weight, trans_in, trans_out, norm_gains)
    sums = block(pair_act.reshape(E, C), cotangent.reshape(E, C), live, *weights)
    out = finish(*sums, *weights)
    return (out[0].reshape(TI, TK, C), *out[1:])


def solution(mesh):
    split = P("row", "col", None)
    in_specs = (split, split, P(), P("row", "col"), P(), P(), P(), P(), P(), P())
    out_specs = (split, P(), P(), P(), P(), P(), P())
    return jax.shard_map(
        on_device, mesh=mesh, in_specs=in_specs, out_specs=out_specs, check_vma=False
    )
```

```python
import functools

import jax
import jax.numpy as jnp
from jax import lax
from jax.experimental import pallas as pl
from jax.experimental.pallas import tpu as pltpu
from jax.sharding import PartitionSpec as P

EPSILON = 1e-05
BF = jnp.bfloat16
F32 = jnp.float32
MESH = pl.DeviceIdType.MESH
C = 128
NR, NQ = 16, 8
ND = NR * NQ
TI, TK = 36, 72
E = TI * TK
NT = 21
EP = NT * 128
MROWS = TI * NR
KP = NQ * 128
MSG = 16
HALF = ND // 2
M_ROWS = 16, 29
G_ROWS = 14, 28
AHEAD = 15
THIRD = 7
VMEM_LIMIT = 60 * 2**20


def vspec(n):
    return [pl.BlockSpec(memory_space=pltpu.VMEM)] * n


def sds(shape, dtype):
    return jax.ShapeDtypeStruct(shape, dtype)


def sigmoid(v):
    return 0.5 * jnp.tanh(0.5 * v) + 0.5


def norm(v):
    center = v - jnp.mean(v, axis=0, keepdims=True)
    inverse = lax.rsqrt(jnp.mean(center * center, axis=0, keepdims=True) + EPSILON)
    return center * inverse, inverse


def norm_back(h, n, inverse):
    first = jnp.mean(h, axis=0, keepdims=True)
    second = jnp.mean(h * n, axis=0, keepdims=True)
    return inverse * (h - first - n * second)


def mm(a, b):
    return jnp.dot(a, b, preferred_element_type=F32)


def mm_nt(a, b):
    return lax.dot_general(a, b, (((1,), (1,)), ((), ())), preferred_element_type=F32)


def eye():
    return (
        lax.broadcasted_iota(jnp.int32, (C, C), 0) == lax.broadcasted_iota(jnp.int32, (C, C), 1)
    ).astype(BF)


def each_peer(fn):
    r, q = lax.axis_index("row"), lax.axis_index("col")

    cols = [lax.rem(q + dq, NQ) for dq in range(NQ)]

    def one(pr, dq):
        fn(pr, cols[dq])

    for dq in range(1, NQ):
        one(r, dq)

    def body(dr, carry):
        pr = lax.rem(r + dr, NR)
        for dq in range(NQ):
            one(pr, dq)
        return carry

    lax.fori_loop(1, NR, body, 0)


def exchange_start(src, dst, src_slot, dst_slot, sems):
    r, q = lax.axis_index("row"), lax.axis_index("col")
    mine = dst_slot(r, q)

    def send(pr, pq):
        pltpu.make_async_remote_copy(
            src_ref=src.at[src_slot(pr, pq)],
            dst_ref=dst.at[mine],
            send_sem=sems.at[0],
            recv_sem=sems.at[1],
            device_id=(pr, pq),
            device_id_type=MESH,
        ).start()

    each_peer(send)
    pltpu.make_async_copy(src.at[src_slot(r, q)], dst.at[mine], sems.at[2]).start()


def exchange_wait(src, dst, sems):
    part = pl.ds(0, ND - 1)
    pltpu.make_async_copy(src.at[part], dst.at[part], sems.at[1]).wait()
    pltpu.make_async_copy(src.at[0], dst.at[0], sems.at[2]).wait()


def exchange_wait_send(src, dst, sems):
    part = pl.ds(0, ND - 1)
    pltpu.make_async_copy(src.at[part], dst.at[part], sems.at[0]).wait()


def by_channel(r, q):
    return r * NQ + q


def by_entry(r, q):
    return q * NR + r


def chunks(count, fn):
    def loop(i, carry):
        fn(i)
        return carry

    lax.fori_loop(0, count, loop, 0)


def widen(src, f_ref, base=0):
    rows = src.shape[1]

    def some(i):
        f_ref[pl.ds(pl.multiple_of(base + i * 16 * rows, 128), 16 * rows), :] = (
            src[pl.ds(i * 16, 16)].astype(F32).reshape(16 * rows, 128)
        )

    chunks(ND // 16, some)


def narrow(f_ref, dst):
    rows = dst.shape[1]

    def some(i):
        dst[pl.ds(i * 16, 16)] = (
            f_ref[pl.ds(pl.multiple_of(i * 16 * rows, 128), 16 * rows), :].reshape(16, rows, 128).astype(BF)
        )

    chunks(ND // 16, some)


def lane_iota():
    return lax.broadcasted_iota(jnp.int32, (8, 128), 1)


def roll(v, shift):
    shift %= 128
    return v if shift == 0 else pltpu.roll(v, shift, 1)


def split_rows(tile, rows):
    lane = lane_iota()
    tiles = {}

    def get(t):
        if t not in tiles:
            tiles[t] = tile(t)
        return tiles[t]

    out = []
    for ii in rows:
        t, l = divmod(TK * ii, 128)
        v = get(t)
        if l + TK > 128:
            v = jnp.where(lane >= l, v, get(t + 1))
        out.append((ii, jnp.where(lane < TK, roll(v, -l), 0.0)))
    return out


def join_rows(row, tiles):
    lane = lane_iota()
    rolled = {}
    out = []
    for t in tiles:
        first = (128 * t) // TK
        final = min((128 * t + 127) // TK, TI - 1)
        value = jnp.zeros((8, 128), F32)
        for ii in range(final, first - 1, -1):
            start = TK * ii - 128 * t
            if ii not in rolled:
                rolled[ii] = roll(row(ii), start)
            if ii == final and start + TK >= 128:
                value = rolled[ii]
            else:
                value = jnp.where(lane < start + TK, rolled[ii], value)
        out.append((t, value))
    return out


def put16(ref, ii, lanes, low, high):
    ref[ii * NR : (ii + 1) * NR, lanes] = jnp.concatenate([low, high], axis=0).astype(BF)


def q_lanes(q):
    return pl.ds(pl.multiple_of(q * 128, 128), 128)


def fold(v):
    return sum(v[:, k : k + 128] for k in range(128, v.shape[1], 128)) + v[:, :128]


def add_blocks(ref, dst):
    total = ref[0].astype(F32)
    for k in range(1, ref.shape[0]):
        total = total + ref[k].astype(F32)
    dst[...] = total.astype(BF)


def block_kernel(
    x_ref, cot_ref, live_ref, pw_ref, gw_ref, ow_ref, ti_ref, to_ref, gain_ref,
    pair_o, mid_sum, tail_sum,
    pwt, gwt, owt, tit, gcol, xt_ref, cott_ref, scaled_ref, proj_ref, gate_ref,
    after_ref, logit_ref, f_ref, fw_ref, l_ref, r_ref, rf_ref, m_ref, mt_ref, c1_ref,
    hid_ref, gi_ref, inner_ref, gh_ref, gp_ref, tin_acc, tout_acc, ow_acc, gw_acc, pw_acc, gn_acc,
    s_a, r_a, s_m0, r_m0, s_m1, r_m1, s_m2, r_m2, s_g0, r_g0, s_g1, r_g1, s_g2, r_g2,
    s_b2, r_b2, s_b3, r_b3,
    s_mid, h_mid, p_mid, r_mid, own_mid,
    s_tail, r_tail, row_tail, q_tail, all_tail,
    sem_a, sem_m, sem_g, sem_b, sem_mid, sem_tail, entered,
):
    H = to_ref.shape[0]
    r, q = lax.axis_index("row"), lax.axis_index("col")
    me = by_channel(r, q)

    barrier = pltpu.get_barrier_semaphore()

    def greet(sem, pr, pq):
        pl.semaphore_signal(sem, inc=1, device_id=(pr, pq), device_id_type=MESH)

    for d in range(1, NQ):
        greet(barrier, r, lax.rem(q + d, NQ))
    for d in range(1, NR):
        greet(barrier, lax.rem(r + d, NR), q)

    def flip(src, dst):
        for b in range(src.shape[1] // C):
            dst[b * C : (b + 1) * C, :] = src[:, b * C : (b + 1) * C].astype(F32).T.astype(BF)

    flip(pw_ref, pwt)
    gcol[...] = jnp.concatenate([gain_ref[...], jnp.zeros((C - 3, C), F32)], axis=0).T
    gain_in, gain_out, gain_t = (lambda: gcol[:, 0:1]), (lambda: gcol[:, 1:2]), (lambda: gcol[:, 2:3])

    def load_t(ref, t0, nt):
        stop = min((t0 + nt) * 128, E)
        rows = ref[t0 * 128 : stop, :]
        pad = (t0 + nt) * 128 - stop
        if pad:
            rows = jnp.concatenate([rows, jnp.zeros((pad, C), rows.dtype)], axis=0)
        return mm_nt(eye(), rows)

    pl.semaphore_wait(barrier, NR + NQ - 2)
    for d in range(1, NQ):
        greet(entered, r, lax.rem(q + d, NQ))

    f_ref[2 * THIRD * C :, :] = jnp.zeros(((MSG - 2 * THIRD) * C, 128), F32)
    for p in range(3):
        for t0, slot, nt in ((p * THIRD, 0, THIRD),):
            lanes = slice(t0 * 128, (t0 + nt) * 128)
            xt = load_t(x_ref, t0, nt)
            xt_ref[:, lanes] = xt.astype(BF)
            scaled = (norm(xt)[0] * gain_in()).astype(BF)
            scaled_ref[:, lanes] = scaled
            proj_ref[:, lanes] = mm(pwt[...], scaled)
            live = live_ref[0:1, lanes]
            for i in range(0, C, 8):
                left = sigmoid(proj_ref[i : i + 8, lanes]) * proj_ref[C + i : C + i + 8, lanes] * live
                right = (
                    sigmoid(proj_ref[2 * C + i : 2 * C + i + 8, lanes])
                    * proj_ref[3 * C + i : 3 * C + i + 8, lanes]
                    * live
                )
                for tt in range(nt):
                    f_ref[(slot + tt) * C + i : (slot + tt) * C + i + 8, :] = left[:, tt * 128 : tt * 128 + 128]
                    row = (THIRD + slot + tt) * C + i
                    f_ref[row : row + 8, :] = right[:, tt * 128 : tt * 128 + 128]

        def pick(i):
            for k in range(8):
                c = i * 8 + k
                s_a[p, c] = jnp.concatenate(
                    [f_ref[pl.ds(c, 8, stride=C), :], f_ref[pl.ds(8 * C + c, 8, stride=C), :]], axis=0
                ).astype(BF)

        chunks(C // 8, pick)
        if p == 0:
            pl.semaphore_wait(entered, NQ - 1)
        exchange_start(s_a.at[p], r_a.at[p], by_channel, by_entry, sem_a.at[p])

    flip(gw_ref, gwt)
    flip(ow_ref, owt)
    flip(ti_ref, tit)
    for ref in (rf_ref, tin_acc, tout_acc, ow_acc, gw_acc, pw_acc, gn_acc):
        ref[...] = jnp.zeros_like(ref)
    for t0 in range(0, NT, THIRD):
        lanes = slice(t0 * 128, (t0 + THIRD) * 128)
        cott_ref[:, lanes] = load_t(cot_ref, t0, THIRD).astype(BF)
        gate_ref[:, lanes] = sigmoid(mm(gwt[...], scaled_ref[:, lanes]))

    for p in range(3):
        exchange_wait(s_a.at[p], r_a.at[p], sem_a.at[p])
        widen(r_a.at[p], fw_ref, p * ND * MSG)

        def per_col(qq):
            def tile(base, row0, stride):
                return lambda t: fw_ref[
                    pl.ds((t // THIRD) * ND * MSG + base * MSG + row0 + t % THIRD, 8, stride=stride), :
                ]

            rows = range(12 * p, 12 * p + 12)
            low = split_rows(tile(qq * NR, 0, MSG), rows)
            high = split_rows(tile(qq * NR + 8, 0, MSG), rows)
            for (ii, a), (_, b) in zip(low, high):
                put16(l_ref, ii, q_lanes(qq), a, b)
            for h in range(2):
                for jj, v in split_rows(tile(qq * NR + h, THIRD, 2 * MSG), rows):
                    rf_ref[pl.ds(qq * KP + h * TI + jj, 8, stride=128), :] = v
            if p == 2:
                r_ref[:, q_lanes(qq)] = rf_ref[pl.ds(pl.multiple_of(qq * KP, KP), KP), :].astype(BF)

        chunks(NQ, per_col)

    m_parts = (
        (0, M_ROWS[0], 0, 8, s_m0, r_m0),
        (M_ROWS[0], M_ROWS[1], 8, 16, s_m1, r_m1),
        (M_ROWS[1], TI, 16, NT, s_m2, r_m2),
    )
    for k, (i0, i1, t0, t1, src, dst) in enumerate(m_parts):
        rows = slice(i0 * NR, i1 * NR)
        size = src.shape[1]
        for b in range(0, KP, 256):
            c1_ref[rows, b : b + 256] = mm_nt(l_ref[rows, :], r_ref[b : b + 256, :])

        def pack(qq):
            for h in range(2):
                row = lambda ii: c1_ref[ii * NR + 8 * h : ii * NR + 8 * h + 8, q_lanes(qq)]
                for t, v in join_rows(row, range(t0, t1)):
                    f_ref[pl.ds((qq * NR + 8 * h) * size + t - t0, 8, stride=size), :] = v

        chunks(NQ, pack)
        narrow(f_ref, src)
        exchange_start(src, dst, by_entry, by_channel, sem_m.at[k])

    def middle(t0, nt, base, size, out0, out_size):
        w = nt * 128
        lanes = slice(t0 * 128, t0 * 128 + w)
        mixed = jnp.concatenate(
            [
                jnp.concatenate(
                    [fw_ref[pl.ds(base + tt + 8 * g * size, 8, stride=size), :] for g in range(C // 8)],
                    axis=0,
                )
                for tt in range(nt)
            ],
            axis=1,
        )
        normed_x, r_x = norm(mixed)
        scaled_out = (normed_x * gain_out()).astype(BF)
        output = mm(owt[...], scaled_out)
        gate = gate_ref[:, lanes]
        after = (xt_ref[:, lanes].astype(F32) + gate * output).astype(BF).astype(F32)
        normed_t, r_t = norm(after)
        scaled_t = (normed_t * gain_t()).astype(BF)
        cot_b = cott_ref[:, lanes]
        hid_ref[:, :w] = mm(tit[...], scaled_t)
        gi_ref[:, :w] = mm(to_ref[...], cot_b)
        for i in range(0, H, 16):
            g = hid_ref[i : i + 16, :w]
            u = hid_ref[H + i : H + i + 16, :w]
            gi = gi_ref[i : i + 16, :w]
            sg = sigmoid(g)
            swish = g * sg
            inner_ref[i : i + 16, :w] = (swish * u).astype(BF)
            gh_ref[i : i + 16, :w] = (gi * u * (sg + swish * (1.0 - sg))).astype(BF)
            gh_ref[H + i : H + i + 16, :w] = (gi * swish).astype(BF)
        back_t = mm(ti_ref[...], gh_ref[:, :w])
        tout_acc[...] += mm_nt(inner_ref[:, :w], cot_b)
        tin_acc[...] += mm_nt(gh_ref[:, :w], scaled_t)
        gn_acc[1] += fold(back_t * normed_t)
        grad_after = cot_b.astype(F32) + norm_back(back_t * gain_t(), normed_t, r_t)
        after_ref[:, lanes] = grad_after
        grad_output = (grad_after * gate).astype(BF)
        grad_logit = (grad_after * output * gate * (1.0 - gate)).astype(BF)
        logit_ref[:, lanes] = grad_logit
        gw_acc[...] += mm_nt(scaled_ref[:, lanes], grad_logit)
        ow_acc[...] += mm_nt(scaled_out, grad_output)
        back_x = mm(ow_ref[...], grad_output)
        gn_acc[0] += fold(back_x * normed_x)
        grad_mixed = norm_back(back_x * gain_out(), normed_x, r_x)
        for tt in range(nt):
            for g in range(C // 8):
                f_ref[pl.ds(out0 + tt + 8 * g * out_size, 8, stride=out_size), :] = grad_mixed[
                    8 * g : 8 * g + 8, tt * 128 : (tt + 1) * 128
                ]

    third = ND * 8
    g_parts = ((s_g0, r_g0), (s_g1, r_g1), (s_g2, r_g2))
    for k, (_, _, t0, t1, src, dst) in enumerate(m_parts):
        exchange_wait(src, dst, sem_m.at[k])
        widen(dst, fw_ref, k * third)
        middle(t0, t1 - t0, k * third, 8, 0, 8)
        narrow(f_ref, g_parts[k][0])
        exchange_start(*g_parts[k], by_channel, by_entry, sem_g.at[k])

    for p in range(3):
        exchange_wait_send(s_a.at[p], r_a.at[p], sem_a.at[p])
    s_b0, s_b1, r_b0, r_b1 = s_a.at[0], s_a.at[1], r_a.at[0], r_a.at[1]
    second = ND * MSG

    def operand(i0, i1):
        def per_col(qq):
            def tile(h):
                first = qq * NR + 8 * h

                def get(t):
                    return fw_ref[pl.ds((t // 8) * third + first * 8 + t % 8, 8, stride=8), :]

                return get

            low, high = split_rows(tile(0), range(i0, i1)), split_rows(tile(1), range(i0, i1))
            for (ii, a), (_, b) in zip(low, high):
                put16(m_ref, ii, q_lanes(qq), a, b)

        chunks(NQ, per_col)
        rows = slice(i0 * NR, i1 * NR)
        for b in range(0, KP, 256):
            c1_ref[rows, b : b + 256] = mm(m_ref[rows, :], r_ref[:, b : b + 256])

    def pack_left(tiles, row0, size):
        def pack(qq):
            for h in range(2):
                row = lambda ii: c1_ref[ii * NR + 8 * h : ii * NR + 8 * h + 8, q_lanes(qq)]
                for t, v in join_rows(row, tiles):
                    f_ref[pl.ds((qq * NR + 8 * h) * size + row0 + t - tiles[0], 8, stride=size), :] = v

        chunks(NQ, pack)

    def pack_right(tiles, row0, size):
        def pack(qq):
            for h in range(2):
                row = lambda jj: rf_ref[pl.ds(qq * KP + h * TI + jj, 8, stride=128), :]
                for t, v in join_rows(row, tiles):
                    at = pl.ds((qq * NR + h) * size + row0 + t - tiles[0], 8, stride=2 * size)
                    f_ref[at, :] = v

        chunks(NQ, pack)

    exchange_wait(s_g0, r_g0, sem_g.at[0])
    widen(r_g0, fw_ref)
    operand(0, G_ROWS[0])
    exchange_wait(s_g1, r_g1, sem_g.at[1])
    widen(r_g1, fw_ref, third)
    operand(G_ROWS[0], G_ROWS[1])
    pack_left(range(0, AHEAD), 0, MSG)
    narrow(f_ref, s_b0)
    exchange_start(s_b0, r_b0, by_entry, by_channel, sem_b.at[0])

    core, chip = lax.rem(r, 2), (r // 2) * NQ + q
    sibling = r + 1 - 2 * core

    def put_terms(dst, first, value):
        half, at = divmod(first // MSG, HALF)
        n = value.shape[0] // MSG
        dst[half, at : at + n] = value.astype(BF).reshape(n, MSG, 128)

    def gain_rows(values):
        rows = [jnp.sum(v.T, axis=0, keepdims=True) for v in values]
        return jnp.concatenate(rows + [jnp.zeros((MSG - len(rows), 128), F32)], axis=0)

    put_terms(s_mid, 0, tin_acc[...])
    put_terms(s_mid, 2 * H, tout_acc[...])
    put_terms(s_mid, 3 * H, ow_acc[...])
    put_terms(s_mid, 3 * H + C, gw_acc[...])
    put_terms(s_mid, 3 * H + 2 * C, gain_rows([gn_acc[0], gn_acc[1]]))
    rest = (3 * H + 2 * C) // MSG - HALF + 1
    s_mid[1, rest:] = jnp.zeros((HALF - rest, MSG, 128), BF)

    def to_sibling(src, dst, sems):
        return pltpu.make_async_remote_copy(
            src_ref=src,
            dst_ref=dst,
            send_sem=sems.at[0],
            recv_sem=sems.at[1],
            device_id=(sibling, q),
            device_id_type=MESH,
        )

    def same_core(src, dst, sems, pick):
        cols = [lax.rem(q + d, NQ) for d in range(NQ)]

        def send(pr, pq):
            pltpu.make_async_remote_copy(
                src_ref=src.at[(pr // 2) * NQ + pq] if pick else src,
                dst_ref=dst.at[chip],
                send_sem=sems.at[0],
                recv_sem=sems.at[1],
                device_id=(pr, pq),
                device_id_type=MESH,
            ).start()

        for d in range(1, NQ):
            send(r, cols[d])

        def rows(k):
            for d in range(NQ):
                send(lax.rem(r + 2 * (k + 1), NR), cols[d])

        chunks(NR // 2 - 1, rows)
        pltpu.make_async_copy(src.at[chip] if pick else src, dst.at[chip], sems.at[2]).start()

    def along(axis, src, dst, sems, pick):
        n, at = (NR, r) if axis == "row" else (NQ, q)
        for d in range(1, n):
            peer = lax.rem(at + d, n)
            pltpu.make_async_remote_copy(
                src_ref=src.at[peer] if pick else src,
                dst_ref=dst.at[at],
                send_sem=sems.at[0],
                recv_sem=sems.at[1],
                device_id=(peer, q) if axis == "row" else (r, peer),
                device_id_type=MESH,
            ).start()
        pltpu.make_async_copy(src.at[at] if pick else src, dst.at[at], sems.at[2]).start()

    def along_wait(dst, sems):
        part = dst.at[pl.ds(0, dst.shape[0] - 1)]
        pltpu.make_async_copy(part, part, sems.at[1]).wait()
        pltpu.make_async_copy(dst.at[0], dst.at[0], sems.at[2]).wait()

    def along_wait_send(dst, sems):
        part = dst.at[pl.ds(0, dst.shape[0] - 1)]
        pltpu.make_async_copy(part, part, sems.at[0]).wait()

    to_sibling(s_mid.at[1 - core], h_mid, sem_mid.at[0]).start()

    exchange_wait(s_g2, r_g2, sem_g.at[2])
    widen(r_g2, fw_ref, 2 * third)
    operand(G_ROWS[1], TI)
    for b in range(0, KP, 128):
        mt_ref[b : b + 128, :] = mm_nt(eye(), m_ref[:, b : b + 128]).astype(BF)
    for b in range(0, KP, 256):
        both = mm(mt_ref[...], l_ref[:, b : b + 256])
        rf_ref[b // 128 * KP : (b // 128 + 1) * KP, :] = both[:, :128]
        rf_ref[(b // 128 + 1) * KP : (b // 128 + 2) * KP, :] = both[:, 128:]
    pack_left(range(AHEAD, NT), 0, MSG)
    pack_right(range(0, 10), NT - AHEAD, MSG)
    narrow(f_ref, s_b1)
    exchange_start(s_b1, r_b1, by_entry, by_channel, sem_b.at[1])
    pack_right(range(10, 18), 0, 8)
    narrow(f_ref, s_b2)
    exchange_start(s_b2, r_b2, by_entry, by_channel, sem_b.at[2])
    pack_right(range(18, NT), 0, 8)
    narrow(f_ref, s_b3)
    exchange_start(s_b3, r_b3, by_entry, by_channel, sem_b.at[3])

    to_sibling(s_mid.at[1 - core], h_mid, sem_mid.at[0]).wait()

    def pair_sum(i):
        at = pl.ds(i * 16, 16)
        p_mid[at] = (s_mid[core, at].astype(F32) + h_mid[at].astype(F32)).astype(BF)

    chunks(HALF // 16, pair_sum)
    same_core(p_mid, r_mid, sem_mid.at[1], True)

    def left_at(t):
        return (t, MSG) if t < AHEAD else (second + t - AHEAD, MSG)

    def right_at(t):
        if t < 10:
            return (second + NT - AHEAD + t, MSG)
        return (2 * second + t - 10, 8) if t < 18 else (2 * second + third + t - 18, 8)

    def project_back(t0, nt):
        w = nt * 128
        lanes = slice(t0 * 128, t0 * 128 + w)
        live = live_ref[0:1, lanes]
        for i in range(0, C, 16):
            for k, at in ((0, left_at), (2, right_at)):
                grad = []
                for t in range(t0, t0 + nt):
                    base, size = at(t)
                    grad.append(
                        jnp.concatenate(
                            [fw_ref[pl.ds(base + (i + 8 * g) * size, 8, stride=size), :] for g in range(2)],
                            axis=0,
                        )
                    )
                s = sigmoid(proj_ref[k * C + i : k * C + i + 16, lanes])
                gs = live * jnp.concatenate(grad, axis=1) * s
                gp_ref[(k + 1) * C + i : (k + 1) * C + i + 16, :w] = gs.astype(BF)
                gp_ref[k * C + i : k * C + i + 16, :w] = (
                    gs * proj_ref[(k + 1) * C + i : (k + 1) * C + i + 16, lanes] * (1.0 - s)
                ).astype(BF)
        normed, inverse = norm(xt_ref[:, lanes].astype(F32))
        pw_acc[...] += mm_nt(gp_ref[:, :w], scaled_ref[:, lanes])
        back = mm(pw_ref[...], gp_ref[:, :w]) + mm(gw_ref[...], logit_ref[:, lanes])
        gn_acc[2] += fold(back * normed)
        after_ref[:, lanes] += norm_back(back * gain_in(), normed, inverse)

    exchange_wait(s_b0, r_b0, sem_b.at[0])
    widen(r_b0, fw_ref)
    exchange_wait(s_b1, r_b1, sem_b.at[1])
    widen(r_b1, fw_ref, second)
    project_back(0, 8)
    exchange_wait(s_b2, r_b2, sem_b.at[2])
    widen(r_b2, fw_ref, 2 * second)
    project_back(8, 8)
    along_wait(r_mid, sem_mid.at[1])
    add_blocks(r_mid, own_mid)
    same_core(own_mid, mid_sum.at[core], sem_mid.at[2], False)
    exchange_wait(s_b3, r_b3, sem_b.at[3])
    widen(r_b3, fw_ref, 2 * second + ND * 8)
    project_back(16, 5)

    own_rows = 4 * C // NR
    s_tail[:, 0:own_rows, :] = pw_acc[...].astype(BF).reshape(NR, own_rows, 128)
    last_gain = gain_rows([gn_acc[2]]).astype(BF)
    for k in range(NR):
        s_tail[k, own_rows : own_rows + MSG, :] = last_gain
    along("row", s_tail, r_tail, sem_tail.at[0], True)

    def pair_rows(t0):
        stop = min((t0 + 3) * 128, E)
        pair_o[t0 * 128 : stop, :] = after_ref[:, t0 * 128 : t0 * 128 + 384].T[: stop - t0 * 128].astype(BF)

    pair_rows(0)
    pair_rows(3)
    along_wait(r_tail, sem_tail.at[0])
    add_blocks(r_tail, row_tail)
    along("col", row_tail, q_tail, sem_tail.at[1], False)
    along_wait(mid_sum.at[core], sem_mid.at[2])
    to_sibling(mid_sum.at[core], mid_sum.at[core], sem_mid.at[3]).start()
    pair_rows(6)
    pair_rows(9)
    pair_rows(12)
    along_wait(q_tail, sem_tail.at[1])
    add_blocks(q_tail, all_tail)
    along("row", all_tail, tail_sum, sem_tail.at[2], False)
    pair_rows(15)
    pair_rows(18)
    to_sibling(mid_sum.at[core], mid_sum.at[core], sem_mid.at[3]).wait()
    along_wait(tail_sum, sem_tail.at[2])


    for k, (_, _, _, _, src, dst) in enumerate(m_parts):
        exchange_wait_send(src, dst, sem_m.at[k])
    for k, (src, dst) in enumerate(g_parts):
        exchange_wait_send(src, dst, sem_g.at[k])
    for k, (src, dst) in enumerate(((s_b0, r_b0), (s_b1, r_b1), (s_b2, r_b2), (s_b3, r_b3))):
        exchange_wait_send(src, dst, sem_b.at[k])
    along_wait_send(r_mid, sem_mid.at[1])
    along_wait_send(mid_sum.at[core], sem_mid.at[2])
    for k, dst in enumerate((r_tail, q_tail, tail_sum)):
        along_wait_send(dst, sem_tail.at[k])


def block(x, cot, live, pw, gw, ow, ti, to, gains):
    H = to.shape[0]
    wide = 1024
    tail = pw.shape[1] // NR + MSG
    msgs = lambda rows, *lead: pltpu.VMEM((*lead, ND, rows, 128), BF)
    dma = lambda *shape: pltpu.SemaphoreType.DMA(shape)
    v = pltpu.VMEM
    return pl.pallas_call(
        block_kernel,
        out_shape=(sds((E, C), BF), sds((2, HALF, MSG, 128), BF), sds((NR, tail, 128), BF)),
        in_specs=vspec(9),
        out_specs=tuple(vspec(3)),
        scratch_shapes=[
            v((4 * C, C), BF), v((C, C), BF), v((C, C), BF), v((2 * H, C), BF), v((C, C), F32),
            v((C, EP), BF), v((C, EP), BF), v((C, EP), BF), v((4 * C, EP), F32), v((C, EP), F32),
            v((C, EP), F32), v((C, EP), BF),
            v((ND * MSG, 128), F32), v((3 * ND * MSG, 128), F32),
            v((MROWS, KP), BF), v((KP, KP), BF), v((NQ * KP, 128), F32), v((MROWS, KP), BF),
            v((KP, MROWS), BF), v((MROWS, KP), F32),
            v((2 * H, wide), F32), v((H, wide), F32), v((H, wide), BF), v((2 * H, wide), BF),
            v((4 * C, wide), BF),
            v((2 * H, C), F32), v((H, C), F32), v((C, C), F32), v((C, C), F32), v((4 * C, C), F32),
            v((3, C, 128), F32),
            msgs(16, 3), msgs(16, 3), *[msgs(8)] * 16,
            v((2, HALF, MSG, 128), BF), v((HALF, MSG, 128), BF), v((HALF, MSG, 128), BF),
            v((HALF, MSG, 128), BF), v((MSG, 128), BF),
            v((NR, tail, 128), BF), v((NR, tail, 128), BF), v((tail, 128), BF), v((NQ, tail, 128), BF),
            v((tail, 128), BF),
            dma(3, 3), dma(3, 3), dma(3, 3), dma(4, 3), dma(4, 3), dma(3, 3),
            pltpu.SemaphoreType.REGULAR,
        ],
        compiler_params=pltpu.CompilerParams(
            collective_id=1, has_side_effects=True, vmem_limit_bytes=VMEM_LIMIT
        ),
        name="block",
    )(x, cot, live, pw, gw, ow, ti, to, gains)


def finish_kernel(pair_ref, mid_ref, tail_ref, pair_o, pw_o, gw_o, ow_o, ti_o, to_o, gn_o):
    H = to_o.shape[0]
    scale = 1.0 / (TI * NR)

    def mid(first, rows):
        half, at = divmod(first // MSG, HALF)
        return mid_ref[half, at : at + rows // MSG].astype(F32).reshape(rows, 128) * scale

    pair_o[...] = pair_ref[...]
    for b in range(0, 2 * H, C):
        ti_o[:, b : b + C] = mid(b, C).T
    to_o[...] = mid(2 * H, H)
    ow_o[...] = mid(3 * H, C)
    gw_o[...] = mid(3 * H + C, C)
    own_rows = 4 * C // NR
    blocks = C // own_rows
    for b in range(4):
        pw = tail_ref[b * blocks : (b + 1) * blocks, 0:own_rows, :].astype(F32).reshape(C, 128)
        pw_o[:, b * C : (b + 1) * C] = pw.T * scale
    last_gain = tail_ref[0, own_rows : own_rows + MSG, :].astype(F32)[0:1] * scale
    gn_o[...] = jnp.concatenate([last_gain, mid(3 * H + 2 * C, MSG)[0:2]], axis=0)


def finish(pair, mid, tail, pw, gw, ow, ti, to, gains):
    return pl.pallas_call(
        finish_kernel,
        out_shape=(
            sds((E, C), BF), sds(pw.shape, F32), sds(gw.shape, F32), sds(ow.shape, F32),
            sds(ti.shape, F32), sds(to.shape, F32), sds(gains.shape, F32),
        ),
        in_specs=vspec(3),
        out_specs=tuple(vspec(7)),
        name="finish",
    )(pair, mid, tail)


def on_device(
    pair_act, cotangent, residue_mask, pair_mask, proj_weight, gate_weight, out_weight,
    trans_in, trans_out, norm_gains,
):
    live_res = residue_mask.astype(F32)
    row_live = lax.dynamic_slice_in_dim(live_res, lax.axis_index("row") * TI, TI)
    col_live = lax.dynamic_slice_in_dim(live_res, lax.axis_index("col") * TK, TK)
    live = pair_mask.astype(F32) * row_live[:, None] * col_live[None, :]
    live = jnp.pad(live.reshape(1, E), ((0, 7), (0, EP - E)))
    weights = (proj_weight, gate_weight, out_weight, trans_in, trans_out, norm_gains)
    sums = block(pair_act.reshape(E, C), cotangent.reshape(E, C), live, *weights)
    out = finish(*sums, *weights)
    return (out[0].reshape(TI, TK, C), *out[1:])


def solution(mesh):
    split = P("row", "col", None)
    in_specs = (split, split, P(), P("row", "col"), P(), P(), P(), P(), P(), P())
    out_specs = (split, P(), P(), P(), P(), P(), P())
    return jax.shard_map(
        on_device, mesh=mesh, in_specs=in_specs, out_specs=out_specs, check_vma=False
    )
```
